32 devices in a mesh: row: 4 (over y, x), col: 8 (over z, core).
Axes of the slice: x: 2, y: 2, z: 4, core: 2. Of those that a mesh axis runs over, the one named last changes fastest.
Arguments:
- ray_feat: bfloat16 [6144, 256], P(('row', 'col'))
- ray_pos: int32 [6144], P(('row', 'col')), may hold values from 0 to 6143, as said below
- target_index: int32 [6144], P(('row', 'col')), may hold values from 0 to 8191
- target_map: bfloat16 [8192, 256], replicated, may hold values from -6 to 6
Outputs:
- feature_grad: float32 [6144, 256], P(('row', 'col'))
The draws below stay inside these ranges and needn't reach their ends.
Inputs may be any that keep to these rules, and one draw needn't show every extreme that they name: `ray_pos`: each position appears once. Cut positions into cells of 192 in order and rays into shards of 192 in order, both numbered row-major over the mesh (row, col); the ray shard of device (r, c) holds exactly 24 positions of every cell of row r and none of other rows.
All inputs are finite; a program needn't handle non-finite values.
Results may differ from the reference program's by a relative error of at most 0.0095.
Values may be sent and summed in bfloat16 or wider, within the bound.
No kernel may reach another device: no remote copies, remote signals or barrier semaphores. Data moves between devices by JAX's collectives and lax.ppermute only.
A program may use at most 64 MiB of HBM per device.

```python
import math
import jax
import jax.numpy as jnp
from jax import lax

C = 256
POS_DEV = 192
TGT = 8192
CELLS = 32
NPOS = 6144
QB = 1536
PAIR = 24


def ray_layout(key):
    col_count = QB // POS_DEV
    cell_keys = jax.random.split(jax.random.fold_in(key, 11), CELLS)
    cell_perms = jax.vmap(lambda item_key: jax.random.permutation(item_key, POS_DEV))(cell_keys)
    device = jnp.arange(CELLS, dtype=jnp.int32)[:, None]
    slot_ids = jnp.arange(POS_DEV, dtype=jnp.int32)[None, :]
    row_block = device // col_count
    column = device % col_count
    owner_cell = row_block * col_count + slot_ids // PAIR
    within = column * PAIR + slot_ids % PAIR
    offsets = cell_perms[owner_cell, within]
    positions = owner_cell * POS_DEV + offsets
    shuffle_keys = jax.random.split(jax.random.fold_in(key, 12), CELLS)
    shuffles = jax.vmap(lambda item_key: jax.random.permutation(item_key, POS_DEV))(shuffle_keys)
    positions = jnp.take_along_axis(positions, shuffles, axis=1)
    return positions.reshape(NPOS).astype(jnp.int32)


def draw_ray_pos(key, part):
    return ray_layout(key)


def draw_ray_feat(key, part):
    positions = ray_layout(key)
    row_count = NPOS // QB
    level = (positions // QB).astype(jnp.float32) / max(row_count - 1, 1)
    common = jax.random.normal(jax.random.fold_in(key, 21), (C,), jnp.float32)
    noise = jax.random.normal(jax.random.fold_in(key, 22), (NPOS, C), jnp.float32)
    spread = jnp.exp(jax.random.uniform(jax.random.fold_in(key, 23), (NPOS, 1), jnp.float32, 0.0, 1.39))
    lift = 2.0 * level
    feats = (noise + lift[:, None] * common[None, :]) * spread
    return feats.astype(jnp.bfloat16)


def set_ends(result, rng, low, top_value):
    shape = result.shape
    index_at = [jax.random.randint(jax.random.fold_in(rng, axis), (), 0, shape[axis]) for axis in range(len(shape))]
    result = result.at[tuple(index_at)].set(low)
    longest = shape.index(max(shape))
    index_at[longest] = (index_at[longest] + 1) % shape[longest]
    return result.at[tuple(index_at)].set(top_value)


def gaussian(own_key, dims, scale, limit, held_as=jnp.bfloat16):
    entries = jax.random.normal(own_key, dims, jnp.float32) * scale
    return jnp.minimum(jnp.maximum(entries, -limit), limit).astype(held_as)


def setup_inputs(seed: int = 0) -> dict:
    streams_of = jax.random.split(jax.random.key(seed), 5)
    ray_feat = draw_ray_feat(jax.random.fold_in(streams_of[4], 71), 0)
    ray_pos = draw_ray_pos(jax.random.fold_in(streams_of[4], 71), 0)
    target_index = set_ends(jax.random.randint(streams_of[2], (NPOS,), 0, TGT), jax.random.fold_in(streams_of[2], 1), 0, TGT - 1).astype(jnp.int32)
    target_map = gaussian(streams_of[3], (TGT, C), 1.0, 6.0)
    return dict(ray_feat=ray_feat, ray_pos=ray_pos, target_index=target_index, target_map=target_map)


normalized_exponent_heat = 0.25
epsilon = 1e-06

def normalize(values):
    as_float = values.astype(jnp.float32)
    norms = jnp.sqrt(lax.optimization_barrier(jnp.sum(as_float * as_float, axis=1, keepdims=True)) + epsilon)
    return ((as_float / norms).astype(jnp.bfloat16), norms)

def reduce_leading_dims(left, right):
    return lax.dot_general(left, right, (((1,), (1,)), ((), ())), preferred_element_type=jnp.float32)

def reference(ray_feat, ray_pos, target_index, target_map):
    render = jnp.zeros_like(ray_feat).at[ray_pos].set(ray_feat)
    normed_directions_leading, norm_x = normalize(render)
    normed_directions_trailing, _ = normalize(jnp.take(target_map, target_index, axis=0))
    block_rows = math.gcd(NPOS, 512)
    block_count = NPOS // block_rows
    x_blocks = normed_directions_leading.reshape(block_count, block_rows, C)
    y_blocks = normed_directions_trailing.reshape(block_count, block_rows, C)

    def affinities(leading_tile_part, trailing_tile_part):
        drawn_kinship = jnp.exp(reduce_leading_dims(leading_tile_part, normed_directions_leading) / normalized_exponent_heat)
        goal_kinship = jnp.exp(reduce_leading_dims(trailing_tile_part, normed_directions_trailing) / normalized_exponent_heat)
        return (drawn_kinship, goal_kinship)

    def first_pass(totals, pieces):
        drawn_kinship, goal_kinship = affinities(pieces[0], pieces[1])
        return ((totals[0] + lax.optimization_barrier(jnp.sum(drawn_kinship, 0)), totals[1] + lax.optimization_barrier(jnp.sum(goal_kinship, 0)), totals[2] + lax.optimization_barrier(jnp.sum(drawn_kinship * drawn_kinship, 0)), totals[3] + lax.optimization_barrier(jnp.sum(drawn_kinship * goal_kinship, 0))), None)
    empty = jnp.zeros((NPOS,), jnp.float32)
    stats, _ = lax.scan(first_pass, (empty, empty, empty, empty), (x_blocks, y_blocks))
    render_sum, target_sum, render_sq, cross_sum = stats
    blend_component = render_sq / (render_sum * render_sum) - cross_sum / (render_sum * target_sum)
    couple_multiplier = float(NPOS) ** 2

    def second_pass(key_part, pieces):
        drawn_kinship, goal_kinship = affinities(pieces[0], pieces[1])
        likelihood_leading = drawn_kinship / render_sum
        likelihood_trailing = goal_kinship / target_sum
        penalty_factor = (couple_multiplier * likelihood_leading * (likelihood_leading - likelihood_trailing - blend_component) / normalized_exponent_heat).astype(jnp.bfloat16)
        query_piece = jnp.dot(penalty_factor, normed_directions_leading, preferred_element_type=jnp.float32)
        key_part = key_part + lax.dot_general(penalty_factor, pieces[0], (((0,), (0,)), ((), ())), preferred_element_type=jnp.float32)
        return (key_part, query_piece)
    key_part, query_pieces = lax.scan(second_pass, jnp.zeros((NPOS, C), jnp.float32), (x_blocks, y_blocks))
    gradient = query_pieces.reshape(NPOS, C) + key_part
    unit_float = normed_directions_leading.astype(jnp.float32)
    return (gradient - unit_float * lax.optimization_barrier(jnp.sum(unit_float * gradient, axis=1, keepdims=True))) / norm_x
```

```python
import functools
import math

import jax
import jax.numpy as jnp
from jax import lax
from jax.experimental import pallas as pl
from jax.experimental.pallas import tpu as pltpu
from jax.sharding import PartitionSpec as P

HEAT = 0.25
EPSILON = 1e-06
EXTRA = 16
BASE = 128
F32 = jnp.float32
BF16 = jnp.bfloat16
VMEM = pl.BlockSpec(memory_space=pltpu.VMEM)
SMEM = pl.BlockSpec(memory_space=pltpu.SMEM)
HIGH = lax.Precision.HIGHEST


def params(mib):
    return pltpu.CompilerParams(vmem_limit_bytes=mib * 2**20)


def unit_rows(values):
    as_float = values.astype(F32)
    norms = jnp.sqrt(jnp.sum(as_float * as_float, axis=1, keepdims=True) + EPSILON)
    return (as_float * (1.0 / norms)).astype(BF16), norms


def widen(table_ref, wide_ref):
    step = math.gcd(table_ref.shape[0], 256)

    @pl.loop(0, table_ref.shape[0] // step)
    def _(i):
        rows = pl.ds(pl.multiple_of(i * step, step), step)
        wide_ref[rows, :] = table_ref[rows, :].astype(F32)


def own_target_kernel(index_ref, table_ref, out_ref, wide_ref, rows_ref):
    widen(table_ref, wide_ref)

    @pl.loop(0, out_ref.shape[0] // 8)
    def _(i):
        rows = [wide_ref[pl.ds(index_ref[i * 8 + j], 1), :] for j in range(8)]
        rows_ref[pl.ds(pl.multiple_of(i * 8, 8), 8), :] = jnp.concatenate(rows, axis=0)

    out_ref[...] = unit_rows(rows_ref[...])[0]


def pick_kernel(count, col_ref, *refs):
    blocks = refs[:count]
    unit_ref, place_ref, target_ref, cell_ref, norm_ref = refs[count:]
    per_device, channels = cell_ref.shape
    me = col_ref[0]
    slot = lax.broadcasted_iota(jnp.int32, (per_device, per_device), 0)
    cell = jnp.zeros((per_device, channels), F32)
    for i, block in enumerate(blocks):
        feats = block[0:per_device, :]
        digits = block[per_device : per_device + EXTRA, :].astype(F32).astype(jnp.int32)
        column, offset, high, low = (digits[k : k + 1, :] for k in range(4))
        place_ref[i : i + 1, :] = (column ^ me) * channels + offset
        target_ref[i : i + 1, :] = high * BASE + low
        wanted = jnp.where(column == me, offset, -1)[:, :per_device]
        chosen = jnp.where(slot == wanted, 1.0, 0.0).astype(BF16)
        cell = cell + jnp.dot(chosen, feats, preferred_element_type=F32)
        unit_ref[i * per_device : (i + 1) * per_device, :] = unit_rows(feats)[0]
    unit, norms = unit_rows(cell.astype(BF16))
    cell_ref[...] = unit
    norm_ref[...] = jnp.broadcast_to(norms, norm_ref.shape)


def query_target_kernel(place_ref, target_ref, table_ref, out_ref, wide_ref, rows_ref):
    widen(table_ref, wide_ref)
    count, channels = place_ref.shape
    per_device = out_ref.shape[0] // count
    shift = channels.bit_length() - 1

    @pl.loop(0, count)
    def _(block):
        @pl.loop(0, per_device // 8)
        def _(i):
            rows = []
            for j in range(8):
                place = place_ref[block, i * 8 + j]
                target = target_ref[place >> shift, place & (channels - 1)]
                rows.append(wide_ref[pl.ds(target, 1), :])
            start = pl.multiple_of(block * per_device + i * 8, 8)
            rows_ref[pl.ds(start, 8), :] = jnp.concatenate(rows, axis=0)

    @pl.loop(0, count)
    def _(block):
        span = pl.ds(pl.multiple_of(block * per_device, 16), per_device)
        out_ref[span, :] = unit_rows(rows_ref[span, :])[0]


def affinity(left, right):
    product = lax.dot_general(
        left, right, (((1,), (1,)), ((), ())), preferred_element_type=F32
    )
    return jnp.exp2(product * (math.log2(math.e) / HEAT))


def lanes_of(length):
    return math.gcd(length, 256)


def fold(values):
    total = values[:, :128]
    for start in range(128, values.shape[1], 128):
        total = total + values[:, start : start + 128]
    return total


def gather_keys(blocks, whole_ref):
    per_device = blocks[0].shape[0]
    for i, block in enumerate(blocks):
        whole_ref[i * per_device : (i + 1) * per_device, :] = block[...]


def stat_kernel(count, qx_ref, qy_ref, *refs):
    kx_blocks, ky_blocks = refs[:count], refs[count : 2 * count]
    key_ref, query_ref, kx_ref, ky_ref, sums_ref = refs[2 * count :]
    gather_keys(kx_blocks, kx_ref)
    gather_keys(ky_blocks, ky_ref)
    sums_ref[...] = jnp.zeros_like(sums_ref)
    lanes = lanes_of(qx_ref.shape[0])

    @pl.loop(0, qx_ref.shape[0] // lanes)
    def _(i):
        span = pl.ds(pl.multiple_of(i * lanes, lanes), lanes)
        render = affinity(kx_ref[...], qx_ref[span, :])
        target = affinity(ky_ref[...], qy_ref[span, :])
        for k, values in enumerate((render, target, render * render, render * target)):
            sums_ref[k] += fold(values)
            query_ref[k : k + 1, span] = jnp.sum(values, axis=0, keepdims=True)

    ones = jnp.ones((8, 128), F32)
    for k in range(4):
        totals = lax.dot_general(
            ones,
            sums_ref[k],
            (((1,), (1,)), ((), ())),
            precision=HIGH,
            preferred_element_type=F32,
        )
        key_ref[k : k + 1, :] = totals[0:1, :]


def factors(sums, scale):
    render, target, square, cross = (sums[k : k + 1, :] for k in range(4))
    by_render, by_target = scale / render, scale / target
    mix = (square * by_render * by_render - cross * by_render * by_target) / scale
    return by_render * by_render, by_render * by_target, by_render * mix


def reorder(values, size, flip):
    blocks = values.shape[1] // size
    return jnp.concatenate(
        [values[:, (i ^ flip) * size : ((i ^ flip) + 1) * size] for i in range(blocks)], axis=1
    )


def sum_pair_kernel(size, own_ref, other_ref, out_ref):
    out_ref[...] = own_ref[...] + reorder(other_ref[...], size, 1)


def grad_kernel(count, parts, scale, qx_ref, qy_ref, *refs):
    kx_blocks, ky_blocks = refs[:count], refs[count : 2 * count]
    refs = refs[2 * count :]
    key_sums, query_sums = refs[:count], refs[count : count + parts]
    outs = refs[count + parts : 2 * count + parts]
    kx_ref, ky_ref, key_ref, query_ref, total_ref = refs[2 * count + parts :]
    per_device = kx_blocks[0].shape[0]
    gather_keys(kx_blocks, kx_ref)
    gather_keys(ky_blocks, ky_ref)

    sums = query_sums[0][...]
    for k in range(1, parts):
        sums = sums + reorder(query_sums[k][...], 2 * per_device, k)
    for k, row in enumerate(factors(sums, scale)):
        query_ref[k : k + 1, :] = row
    sums = key_sums[0][...]
    for k in range(1, count):
        sums = sums + reorder(key_sums[k][...], per_device, k)
    for k, row in enumerate(factors(sums, scale)):
        key_ref[k] = jnp.broadcast_to(row, (128, row.shape[1])).T

    total_ref[...] = jnp.zeros_like(total_ref)
    lanes = lanes_of(qx_ref.shape[0])

    @pl.loop(0, qx_ref.shape[0] // lanes)
    def _(i):
        span = pl.ds(pl.multiple_of(i * lanes, lanes), lanes)
        queries = qx_ref[span, :]
        render = affinity(kx_ref[...], queries)
        target = affinity(ky_ref[...], qy_ref[span, :])
        weights = []
        for start in range(0, lanes, 128):
            part = slice(start, start + 128)
            at = pl.ds(pl.multiple_of(i * lanes + start, 128), 128)
            square, cross, single = (key_ref[k] + query_ref[k : k + 1, at] for k in range(3))
            a, b = render[:, part], target[:, part]
            weights.append((a * (a * square - b * cross - single)).astype(BF16))
        total_ref[...] += jnp.dot(
            jnp.concatenate(weights, axis=1), queries, preferred_element_type=F32
        )

    for k, out in enumerate(outs):
        out[...] = total_ref[k * per_device : (k + 1) * per_device, :].astype(out.dtype)


def last_kernel(unit_ref, norm_ref, *refs):
    parts, out_ref = refs[:-1], refs[-1]
    gradient = parts[0][...]
    for part in parts[1:]:
        gradient = gradient + part[...].astype(F32)
    unit = unit_ref[...].astype(F32)
    along = jnp.sum(unit * gradient, axis=1, keepdims=True)
    out_ref[...] = (gradient - unit * along) / norm_ref[:, :1]


def call(kernel, out_shape, args, in_specs=None, scratch=(), mib=16, flops=0, nbytes=0):
    many = isinstance(out_shape, (tuple, list))
    return pl.pallas_call(
        kernel,
        out_shape=out_shape,
        in_specs=in_specs or [VMEM] * len(args),
        out_specs=[VMEM] * len(out_shape) if many else VMEM,
        scratch_shapes=scratch,
        compiler_params=params(mib),
        cost_estimate=pl.CostEstimate(flops=flops, bytes_accessed=nbytes, transcendentals=0),
    )(*args)


def body(ray_feat, ray_pos, target_index, target_map):
    per_device, channels = ray_feat.shape
    col_count = lax.axis_size("col")
    row_count = lax.axis_size("row")
    shape = jax.ShapeDtypeStruct
    queries, keys = col_count * per_device, row_count * per_device

    def flip(values, axis, bits):
        pairs = [(i, i ^ bits) for i in range(lax.axis_size(axis))]
        return lax.ppermute(values, axis, pairs)

    digits = jnp.stack(
        [
            ray_pos // per_device % col_count,
            ray_pos % per_device,
            target_index // BASE,
            target_index % BASE,
        ]
    )
    digits = jnp.pad(digits, ((0, EXTRA - 4), (0, channels - per_device)))
    sent = jnp.concatenate([ray_feat, digits.astype(F32).astype(BF16)], axis=0)
    blocks = []
    for k in range(col_count // 2):
        block = flip(sent, "col", 2 * k) if k else sent
        blocks += [block, flip(block, "col", 1)]

    own_target = call(
        own_target_kernel,
        shape((per_device, channels), BF16),
        (target_index, target_map),
        in_specs=[SMEM, VMEM],
        scratch=[pltpu.VMEM(target_map.shape, F32), pltpu.VMEM((per_device, channels), F32)],
        mib=24,
        nbytes=target_map.size * 2,
    )
    key_targets = [own_target] + [flip(own_target, "row", k) for k in range(1, row_count)]

    me = lax.axis_index("col").astype(jnp.int32).reshape(1)
    query_unit, places, targets, own_unit, own_norm = call(
        functools.partial(pick_kernel, col_count),
        (
            shape((queries, channels), BF16),
            shape((col_count, channels), jnp.int32),
            shape((col_count, channels), jnp.int32),
            shape((per_device, channels), BF16),
            shape((per_device, 128), F32),
        ),
        (me, *blocks),
        in_specs=[SMEM] + [VMEM] * col_count,
        nbytes=queries * channels * 4,
    )
    key_units = [own_unit] + [flip(own_unit, "row", k) for k in range(1, row_count)]
    query_target = call(
        query_target_kernel,
        shape((queries, channels), BF16),
        (places, targets, target_map),
        in_specs=[SMEM, SMEM, VMEM],
        scratch=[pltpu.VMEM(target_map.shape, F32), pltpu.VMEM((queries, channels), F32)],
        mib=24,
        nbytes=target_map.size * 4,
    )

    flops = 2 * queries * keys * channels
    key_scratch = [pltpu.VMEM((keys, channels), BF16)] * 2
    key_sums, query_sums = call(
        functools.partial(stat_kernel, row_count),
        (shape((4, keys), F32), shape((4, queries), F32)),
        (query_unit, query_target, *key_units, *key_targets),
        scratch=key_scratch + [pltpu.VMEM((4, keys, 128), F32)],
        mib=32,
        flops=2 * flops,
    )
    key_parts = [key_sums] + [flip(key_sums, "row", k) for k in range(1, row_count)]
    query_sums = call(
        functools.partial(sum_pair_kernel, per_device),
        shape((4, queries), F32),
        (query_sums, flip(query_sums, "col", 1)),
    )
    query_parts = [query_sums] + [
        flip(query_sums, "col", 2 * k) for k in range(1, col_count // 2)
    ]
    scale = float(queries * row_count) / math.sqrt(HEAT)
    partials = call(
        functools.partial(grad_kernel, row_count, len(query_parts), scale),
        [shape((per_device, channels), F32 if k == 0 else BF16) for k in range(row_count)],
        (query_unit, query_target, *key_units, *key_targets, *key_parts, *query_parts),
        scratch=key_scratch
        + [
            pltpu.VMEM((3, keys, 128), F32),
            pltpu.VMEM((3, queries), F32),
            pltpu.VMEM((keys, channels), F32),
        ],
        mib=32,
        flops=3 * flops,
    )
    partials = [partials[0]] + [flip(partials[k], "row", k) for k in range(1, row_count)]
    return call(
        last_kernel,
        shape((per_device, channels), F32),
        (own_unit, own_norm, *partials),
    )


def solution(mesh):
    return jax.shard_map(
        body,
        mesh=mesh,
        in_specs=(P(("row", "col"), None), P(("row", "col")), P(("row", "col")), P()),
        out_specs=P(("row", "col"), None),
        check_vma=False,
    )
```

```python
import functools
import math

import jax
import jax.numpy as jnp
from jax import lax
from jax.experimental import pallas as pl
from jax.experimental.pallas import tpu as pltpu
from jax.sharding import PartitionSpec as P

HEAT = 0.25
EPSILON = 1e-06
EXTRA = 16
BASE_BITS = 7
BASE = 1 << BASE_BITS
F32 = jnp.float32
BF16 = jnp.bfloat16
VMEM = pl.BlockSpec(memory_space=pltpu.VMEM)
SMEM = pl.BlockSpec(memory_space=pltpu.SMEM)
HBM = pl.BlockSpec(memory_space=pltpu.HBM)
FULL = 60
PIECES = 8
HIGH = lax.Precision.HIGHEST


def params(mib):
    return pltpu.CompilerParams(vmem_limit_bytes=mib * 2**20)


def unit_rows(values):
    as_float = values.astype(F32)
    norms = jnp.sqrt(jnp.sum(as_float * as_float, axis=1, keepdims=True) + EPSILON)
    return (as_float * (1.0 / norms)).astype(BF16), norms


def table_scratch(table, rows):
    half = table.shape[1] // 2
    return [
        pltpu.VMEM(table.shape, BF16),
        pltpu.VMEM((2 * table.shape[0], half), F32),
        pltpu.VMEM((2 * rows, half), F32),
        pltpu.SemaphoreType.DMA((PIECES,)),
    ]


def load_table(table_ref, narrow_ref, wide_ref, sems):
    size = table_ref.shape[0] // PIECES
    half = table_ref.shape[1] // 2

    def copy(i):
        rows = pl.ds(i * size, size)
        return pltpu.make_async_copy(table_ref.at[rows, :], narrow_ref.at[rows, :], sems.at[i])

    for i in range(PIECES):
        copy(i).start()
    step = math.gcd(size, 256)
    for i in range(PIECES):
        copy(i).wait()

        @pl.loop(i * (size // step), (i + 1) * (size // step))
        def _(j):
            start = pl.multiple_of(j * step, step)
            values = narrow_ref[pl.ds(start, step), :].astype(F32)
            wide_ref[pl.ds(start * 2, step, 2), :] = values[:, :half]
            wide_ref[pl.ds(start * 2 + 1, step, 2), :] = values[:, half:]


def take_rows(index, start, count, wide_ref, rows_ref):
    @pl.loop(0, count // 32)
    def _(i):
        for group in range(8):
            first = i * 32 + group * 4
            rows = [wide_ref[pl.ds(index(first + j) * 2, 2), :] for j in range(4)]
            at = pl.multiple_of(start * 2 + first * 2, 8)
            rows_ref[pl.ds(at, 8), :] = jnp.concatenate(rows, axis=0)


def unit_taken(rows_ref, out_ref):
    rows, half = out_ref.shape[0], out_ref.shape[1] // 2
    step = math.gcd(rows, 64)
    for start in range(0, rows, step):
        left = rows_ref[pl.ds(2 * start, step, 2), :]
        right = rows_ref[pl.ds(2 * start + 1, step, 2), :]
        square = jnp.sum(left * left + right * right, axis=1, keepdims=True)
        inverse = 1.0 / jnp.sqrt(square + EPSILON)
        out_ref[start : start + step, :half] = (left * inverse).astype(BF16)
        out_ref[start : start + step, half:] = (right * inverse).astype(BF16)


def own_target_kernel(index_ref, table_ref, out_ref, narrow_ref, wide_ref, rows_ref, sems):
    load_table(table_ref, narrow_ref, wide_ref, sems)
    take_rows(lambda i: index_ref[i], 0, out_ref.shape[0], wide_ref, rows_ref)
    unit_taken(rows_ref, out_ref)


def query_target_kernel(per_device, target_ref, table_ref, out_ref, narrow_ref, wide_ref, rows_ref, sems):
    load_table(table_ref, narrow_ref, wide_ref, sems)
    stride = table_ref.shape[1]
    for block in range(out_ref.shape[0] // per_device):
        start = block * stride
        take_rows(lambda i: target_ref[0, start + i], block * per_device, per_device, wide_ref, rows_ref)
    unit_taken(rows_ref, out_ref)


def send_kernel(columns, row_ref, feat_ref, pos_ref, index_ref, out_ref, pos_own, index_own, sems):
    per_device, channels = feat_ref.shape
    copies = [
        pltpu.make_async_copy(pos_ref, pos_own, sems.at[0]),
        pltpu.make_async_copy(index_ref, index_own, sems.at[1]),
        pltpu.make_async_copy(feat_ref, out_ref.at[pl.ds(0, per_device), :], sems.at[2]),
    ]
    for copy in copies:
        copy.start()
    for copy in copies[:2]:
        copy.wait()
    pos, index = pos_own[...] - row_ref[0] * (columns * per_device), index_own[...]
    cell = jnp.zeros_like(pos)
    for k in range(1, columns):
        cell = cell + (pos >= k * per_device).astype(jnp.int32)
    rows = [cell, pos - cell * per_device, index >> BASE_BITS, index & (BASE - 1)]
    digits = jnp.concatenate(rows + [jnp.zeros((EXTRA - 4, per_device), jnp.int32)], axis=0)
    pad = jnp.zeros((EXTRA, channels - per_device), jnp.int32)
    digits = jnp.concatenate([digits, pad], axis=1) if channels > per_device else digits
    out_ref[per_device : per_device + EXTRA, :] = digits.astype(F32).astype(BF16)
    copies[2].wait()


def pick_kernel(count, col_ref, own_ref, *refs):
    blocks = refs[:count]
    unit_ref, target_ref, cell_ref, norm_ref = refs[count:]
    per_device, channels = own_ref.shape
    me = col_ref[0]
    slot = lax.broadcasted_iota(jnp.int32, (per_device, per_device), 0)
    cell = jnp.zeros((per_device, channels), F32)
    digits = [block[per_device : per_device + EXTRA, :] for block in blocks]
    table = jnp.concatenate([d[2:4, :per_device].astype(F32) for d in digits], axis=0).astype(BF16)
    for i, block in enumerate(blocks):
        feats = block[0:per_device, :]
        column, offset = (digits[i][k : k + 1, :per_device].astype(F32).astype(jnp.int32) for k in range(2))
        at_slot = jnp.where(slot == offset, 1.0, 0.0)
        found = jnp.dot(table, at_slot.astype(BF16), preferred_element_type=F32)
        target = jnp.zeros((1, per_device), F32)
        for j in range(count):
            value = found[2 * j : 2 * j + 1, :] * BASE + found[2 * j + 1 : 2 * j + 2, :]
            target = target + jnp.where((column ^ me) == j, value, 0.0)
        target_ref[:, i * channels : i * channels + per_device] = target.astype(jnp.int32)
        chosen = jnp.where(column == me, at_slot, 0.0).astype(BF16)
        cell = cell + jnp.dot(chosen, feats, preferred_element_type=F32)
        unit_ref[i * per_device : (i + 1) * per_device, :] = unit_rows(feats)[0]
    unit, norms = unit_rows(cell.astype(BF16))
    cell_ref[0:per_device, :] = unit
    cell_ref[per_device:, :] = own_ref[...]
    norm_ref[...] = jnp.broadcast_to(norms, norm_ref.shape)


def affinity(left, right):
    product = lax.dot_general(
        left, right, (((1,), (1,)), ((), ())), preferred_element_type=F32
    )
    return jnp.exp2(product * (math.log2(math.e) / HEAT))


def lanes_of(length):
    return math.gcd(length, 256)


def fold(values):
    total = values[:, :128]
    for start in range(128, values.shape[1], 128):
        total = total + values[:, start : start + 128]
    return total


def gather_keys(blocks, whole_refs):
    per_device = blocks[0].shape[0] // 2
    for i, block in enumerate(blocks):
        for k, whole_ref in enumerate(whole_refs):
            whole_ref[i * per_device : (i + 1) * per_device, :] = block[k * per_device : (k + 1) * per_device, :]


def stat_kernel(count, qx_ref, qy_ref, *refs):
    key_ref, query_ref, kx_ref, ky_ref, sums_ref = refs[count:]
    gather_keys(refs[:count], (kx_ref, ky_ref))
    sums_ref[...] = jnp.zeros_like(sums_ref)
    lanes = lanes_of(qx_ref.shape[0])

    @pl.loop(0, qx_ref.shape[0] // lanes)
    def _(i):
        span = pl.ds(pl.multiple_of(i * lanes, lanes), lanes)
        render = affinity(kx_ref[...], qx_ref[span, :])
        target = affinity(ky_ref[...], qy_ref[span, :])
        for k, values in enumerate((render, target, render * render, render * target)):
            sums_ref[k] += fold(values)
            query_ref[k : k + 1, span] = jnp.sum(values, axis=0, keepdims=True)

    ones = jnp.ones((8, 128), F32)
    for k in range(4):
        totals = lax.dot_general(
            ones,
            sums_ref[k],
            (((1,), (1,)), ((), ())),
            precision=HIGH,
            preferred_element_type=F32,
        )
        key_ref[k : k + 1, :] = totals[0:1, :]


def factors(sums, scale):
    render, target, square, cross = (sums[k : k + 1, :] for k in range(4))
    by_render, by_target = scale / render, scale / target
    mix = (square * by_render * by_render - cross * by_render * by_target) / scale
    return by_render * by_render, by_render * by_target, by_render * mix


def reorder(values, size, flip):
    blocks = values.shape[1] // size
    return jnp.concatenate(
        [values[:, (i ^ flip) * size : ((i ^ flip) + 1) * size] for i in range(blocks)], axis=1
    )


def sum_pair_kernel(size, own_ref, other_ref, out_ref):
    out_ref[...] = own_ref[...] + reorder(other_ref[...], size, 1)


def grad_kernel(count, parts, scale, qx_ref, qy_ref, *refs):
    blocks, refs = refs[:count], refs[count:]
    key_sums, query_sums = refs[:count], refs[count : count + parts]
    outs = refs[count + parts : 2 * count + parts]
    kx_ref, ky_ref, key_ref, query_ref, total_ref = refs[2 * count + parts :]
    per_device = blocks[0].shape[0] // 2
    gather_keys(blocks, (kx_ref, ky_ref))

    sums = query_sums[0][...]
    for k in range(1, parts):
        sums = sums + reorder(query_sums[k][...], 2 * per_device, k)
    for k, row in enumerate(factors(sums, scale)):
        query_ref[k : k + 1, :] = row
    sums = key_sums[0][...]
    for k in range(1, count):
        sums = sums + reorder(key_sums[k][...], per_device, k)
    for k, row in enumerate(factors(sums, scale)):
        key_ref[k] = jnp.broadcast_to(row, (128, row.shape[1])).T

    total_ref[...] = jnp.zeros_like(total_ref)
    lanes = lanes_of(qx_ref.shape[0])

    @pl.loop(0, qx_ref.shape[0] // lanes)
    def _(i):
        span = pl.ds(pl.multiple_of(i * lanes, lanes), lanes)
        queries = qx_ref[span, :]
        render = affinity(kx_ref[...], queries)
        target = affinity(ky_ref[...], qy_ref[span, :])
        weights = []
        for start in range(0, lanes, 128):
            part = slice(start, start + 128)
            at = pl.ds(pl.multiple_of(i * lanes + start, 128), 128)
            square, cross, single = (key_ref[k] + query_ref[k : k + 1, at] for k in range(3))
            a, b = render[:, part], target[:, part]
            weights.append((a * (a * square - b * cross - single)).astype(BF16))
        total_ref[...] += jnp.dot(
            jnp.concatenate(weights, axis=1), queries, preferred_element_type=F32
        )

    for k, out in enumerate(outs):
        out[...] = total_ref[k * per_device : (k + 1) * per_device, :].astype(out.dtype)


def last_kernel(unit_ref, norm_ref, *refs):
    parts, out_ref = refs[:-1], refs[-1]
    gradient = parts[0][...]
    for part in parts[1:]:
        gradient = gradient + part[...].astype(F32)
    unit = unit_ref[0 : gradient.shape[0], :].astype(F32)
    along = jnp.sum(unit * gradient, axis=1, keepdims=True)
    out_ref[...] = (gradient - unit * along) / norm_ref[:, :1]


def call(kernel, out_shape, args, in_specs=None, scratch=(), mib=16, flops=0, nbytes=0):
    many = isinstance(out_shape, (tuple, list))
    return pl.pallas_call(
        kernel,
        out_shape=out_shape,
        in_specs=in_specs or [VMEM] * len(args),
        out_specs=[VMEM] * len(out_shape) if many else VMEM,
        scratch_shapes=scratch,
        compiler_params=params(mib),
        cost_estimate=pl.CostEstimate(flops=flops, bytes_accessed=nbytes, transcendentals=0),
    )(*args)


def body(ray_feat, ray_pos, target_index, target_map):
    per_device, channels = ray_feat.shape
    col_count = lax.axis_size("col")
    row_count = lax.axis_size("row")
    shape = jax.ShapeDtypeStruct
    queries, keys = col_count * per_device, row_count * per_device

    def flip(values, axis, bits):
        pairs = [(i, i ^ bits) for i in range(lax.axis_size(axis))]
        return lax.ppermute(values, axis, pairs)

    me = lax.axis_index("col").astype(jnp.int32).reshape(1)
    sent = call(
        functools.partial(send_kernel, col_count),
        shape((per_device + EXTRA, channels), BF16),
        (
            lax.axis_index("row").astype(jnp.int32).reshape(1),
            ray_feat,
            ray_pos.reshape(1, -1),
            target_index.reshape(1, -1),
        ),
        in_specs=[SMEM, HBM, HBM, HBM],
        scratch=[pltpu.VMEM((1, per_device), jnp.int32)] * 2 + [pltpu.SemaphoreType.DMA((3,))],
        mib=FULL,
    )
    own_target = call(
        own_target_kernel,
        shape((per_device, channels), BF16),
        (target_index, target_map),
        in_specs=[SMEM, HBM],
        scratch=table_scratch(target_map, per_device),
        mib=24,
        nbytes=target_map.size * 2,
    )
    blocks = [sent, flip(sent, "col", 1)]
    for k in range(2, col_count, 2):
        block, own_target = lax.optimization_barrier((flip(sent, "col", k), own_target))
        blocks += [block, flip(block, "col", 1)]
    query_unit, targets, own_block, own_norm = call(
        functools.partial(pick_kernel, col_count),
        (
            shape((queries, channels), BF16),
            shape((1, col_count * channels), jnp.int32),
            shape((2 * per_device, channels), BF16),
            shape((per_device, 128), F32),
        ),
        (me, own_target, *blocks),
        in_specs=[SMEM] + [VMEM] * (col_count + 1),
        nbytes=queries * channels * 4,
    )
    key_blocks = [own_block] + [flip(own_block, "row", k) for k in range(1, row_count)]
    query_target = call(
        functools.partial(query_target_kernel, per_device),
        shape((queries, channels), BF16),
        (targets, target_map),
        in_specs=[SMEM, HBM],
        scratch=table_scratch(target_map, queries),
        mib=24,
        nbytes=target_map.size * 2,
    )

    flops = 2 * queries * keys * channels
    key_scratch = [pltpu.VMEM((keys, channels), BF16)] * 2
    key_sums, query_sums = call(
        functools.partial(stat_kernel, row_count),
        (shape((4, keys), F32), shape((4, queries), F32)),
        (query_unit, query_target, *key_blocks),
        scratch=key_scratch + [pltpu.VMEM((4, keys, 128), F32)],
        mib=32,
        flops=2 * flops,
    )
    key_parts = [key_sums] + [flip(key_sums, "row", k) for k in range(1, row_count)]
    query_sums = call(
        functools.partial(sum_pair_kernel, per_device),
        shape((4, queries), F32),
        (query_sums, flip(query_sums, "col", 1)),
    )
    query_parts = [query_sums] + [
        flip(query_sums, "col", 2 * k) for k in range(1, col_count // 2)
    ]
    scale = float(queries * row_count) / math.sqrt(HEAT)
    partials = call(
        functools.partial(grad_kernel, row_count, len(query_parts), scale),
        [shape((per_device, channels), F32 if k == 0 else BF16) for k in range(row_count)],
        (query_unit, query_target, *key_blocks, *key_parts, *query_parts),
        scratch=key_scratch
        + [
            pltpu.VMEM((3, keys, 128), F32),
            pltpu.VMEM((3, queries), F32),
            pltpu.VMEM((keys, channels), F32),
        ],
        mib=32,
        flops=3 * flops,
    )
    partials = [partials[0]] + [flip(partials[k], "row", k) for k in range(1, row_count)]
    return call(
        last_kernel,
        shape((per_device, channels), F32),
        (own_block, own_norm, *partials),
    )


def solution(mesh):
    return jax.shard_map(
        body,
        mesh=mesh,
        in_specs=(P(("row", "col"), None), P(("row", "col")), P(("row", "col")), P()),
        out_specs=P(("row", "col"), None),
        check_vma=False,
    )
```

```python
import functools
import math

import jax
import jax.numpy as jnp
from jax import lax
from jax.experimental import pallas as pl
from jax.experimental.pallas import tpu as pltpu
from jax.sharding import PartitionSpec as P

HEAT = 0.25
EPSILON = 1e-06
EXTRA = 16
BASE_BITS = 7
BASE = 1 << BASE_BITS
F32 = jnp.float32
BF16 = jnp.bfloat16
VMEM = pl.BlockSpec(memory_space=pltpu.VMEM)
SMEM = pl.BlockSpec(memory_space=pltpu.SMEM)
HBM = pl.BlockSpec(memory_space=pltpu.HBM)
FULL = 60
PIECES = 8
HIGH = lax.Precision.HIGHEST


def params(mib):
    return pltpu.CompilerParams(vmem_limit_bytes=mib * 2**20)


def unit_rows(values):
    as_float = values.astype(F32)
    norms = jnp.sqrt(jnp.sum(as_float * as_float, axis=1, keepdims=True) + EPSILON)
    return (as_float * (1.0 / norms)).astype(BF16), norms


def table_scratch(table, rows):
    half = table.shape[1] // 2
    return [
        pltpu.VMEM(table.shape, BF16),
        pltpu.VMEM((2 * table.shape[0], half), F32),
        pltpu.VMEM((2 * rows, half), F32),
        pltpu.SemaphoreType.DMA((PIECES,)),
    ]


def load_table(table_ref, narrow_ref, wide_ref, sems):
    size = table_ref.shape[0] // PIECES
    half = table_ref.shape[1] // 2

    def copy(i):
        rows = pl.ds(i * size, size)
        return pltpu.make_async_copy(table_ref.at[rows, :], narrow_ref.at[rows, :], sems.at[i])

    for i in range(PIECES):
        copy(i).start()
    step = math.gcd(size, 256)
    for i in range(PIECES):
        copy(i).wait()

        @pl.loop(i * (size // step), (i + 1) * (size // step))
        def _(j):
            start = pl.multiple_of(j * step, step)
            values = narrow_ref[pl.ds(start, step), :].astype(F32)
            wide_ref[pl.ds(start * 2, step, 2), :] = values[:, :half]
            wide_ref[pl.ds(start * 2 + 1, step, 2), :] = values[:, half:]


def take_rows(index, start, count, wide_ref, rows_ref):
    @pl.loop(0, count // 32)
    def _(i):
        for group in range(8):
            first = i * 32 + group * 4
            rows = [wide_ref[pl.ds(index(first + j) * 2, 2), :] for j in range(4)]
            at = pl.multiple_of(start * 2 + first * 2, 8)
            rows_ref[pl.ds(at, 8), :] = jnp.concatenate(rows, axis=0)


def unit_taken(rows_ref, out_ref):
    rows, half = out_ref.shape[0], out_ref.shape[1] // 2
    step = math.gcd(rows, 64)
    for start in range(0, rows, step):
        left = rows_ref[pl.ds(2 * start, step, 2), :]
        right = rows_ref[pl.ds(2 * start + 1, step, 2), :]
        square = jnp.sum(left * left + right * right, axis=1, keepdims=True)
        inverse = 1.0 / jnp.sqrt(square + EPSILON)
        out_ref[start : start + step, :half] = (left * inverse).astype(BF16)
        out_ref[start : start + step, half:] = (right * inverse).astype(BF16)


def own_target_kernel(index_ref, table_ref, out_ref, narrow_ref, wide_ref, rows_ref, sems):
    load_table(table_ref, narrow_ref, wide_ref, sems)
    take_rows(lambda i: index_ref[i], 0, out_ref.shape[0], wide_ref, rows_ref)
    unit_taken(rows_ref, out_ref)


def query_target_kernel(per_device, target_ref, table_ref, out_ref, narrow_ref, wide_ref, rows_ref, sems):
    load_table(table_ref, narrow_ref, wide_ref, sems)
    stride = table_ref.shape[1]
    for block in range(out_ref.shape[0] // per_device):
        start = block * stride
        take_rows(lambda i: target_ref[0, start + i], block * per_device, per_device, wide_ref, rows_ref)
    unit_taken(rows_ref, out_ref)


def send_kernel(columns, row_ref, feat_ref, pos_ref, index_ref, out_ref, pos_own, index_own, sems):
    per_device, channels = feat_ref.shape
    copies = [
        pltpu.make_async_copy(pos_ref, pos_own, sems.at[0]),
        pltpu.make_async_copy(index_ref, index_own, sems.at[1]),
        pltpu.make_async_copy(feat_ref, out_ref.at[pl.ds(0, per_device), :], sems.at[2]),
    ]
    for copy in copies:
        copy.start()
    for copy in copies[:2]:
        copy.wait()
    pos, index = pos_own[...] - row_ref[0] * (columns * per_device), index_own[...]
    cell = jnp.zeros_like(pos)
    for k in range(1, columns):
        cell = cell + (pos >= k * per_device).astype(jnp.int32)
    rows = [cell, pos - cell * per_device, index >> BASE_BITS, index & (BASE - 1)]
    digits = jnp.concatenate(rows + [jnp.zeros((EXTRA - 4, per_device), jnp.int32)], axis=0)
    pad = jnp.zeros((EXTRA, channels - per_device), jnp.int32)
    digits = jnp.concatenate([digits, pad], axis=1) if channels > per_device else digits
    out_ref[per_device : per_device + EXTRA, :] = digits.astype(F32).astype(BF16)
    copies[2].wait()


def pick_kernel(count, col_ref, own_ref, *refs):
    blocks = refs[:count]
    unit_ref, target_ref, cell_ref, norm_ref = refs[count:]
    per_device, channels = own_ref.shape
    me = col_ref[0]
    slot = lax.broadcasted_iota(jnp.int32, (per_device, per_device), 0)
    cell = jnp.zeros((per_device, channels), F32)
    digits = [block[per_device : per_device + EXTRA, :] for block in blocks]
    table = jnp.concatenate([d[2:4, :per_device].astype(F32) for d in digits], axis=0).astype(BF16)
    for i, block in enumerate(blocks):
        feats = block[0:per_device, :]
        column, offset = (digits[i][k : k + 1, :per_device].astype(F32).astype(jnp.int32) for k in range(2))
        at_slot = jnp.where(slot == offset, 1.0, 0.0)
        found = jnp.dot(table, at_slot.astype(BF16), preferred_element_type=F32)
        target = jnp.zeros((1, per_device), F32)
        for j in range(count):
            value = found[2 * j : 2 * j + 1, :] * BASE + found[2 * j + 1 : 2 * j + 2, :]
            target = target + jnp.where((column ^ me) == j, value, 0.0)
        target_ref[:, i * channels : i * channels + per_device] = target.astype(jnp.int32)
        chosen = jnp.where(column == me, at_slot, 0.0).astype(BF16)
        cell = cell + jnp.dot(chosen, feats, preferred_element_type=F32)
        unit_ref[i * per_device : (i + 1) * per_device, :] = unit_rows(feats)[0]
    unit, norms = unit_rows(cell.astype(BF16))
    cell_ref[0:per_device, :] = unit
    cell_ref[per_device:, :] = own_ref[...]
    norm_ref[...] = jnp.broadcast_to(norms, norm_ref.shape)


def products(left, right):
    return lax.dot_general(left, right, (((1,), (1,)), ((), ())), preferred_element_type=F32)


def affinity(product):
    return jnp.exp2(product * (math.log2(math.e) / HEAT))


def lanes_of(length):
    return math.gcd(length, 512)


def each_part(length, body):
    size = math.gcd(length, 768)
    if size == length:
        body(0, size)
    else:
        pl.loop(0, length // size)(lambda i: body(pl.multiple_of(i * size, size), size))


def tiles(rows, lanes):
    for strip in range(0, rows, 16):
        yield strip, [
            [(slice(row, row + 8), slice(lane, lane + 128)) for row in range(strip, strip + 16, 8)]
            for lane in range(0, lanes, 128)
        ]


def gather_keys(blocks, whole_refs):
    per_device = blocks[0].shape[0] // 2
    for i, block in enumerate(blocks):
        for k, whole_ref in enumerate(whole_refs):
            whole_ref[i * per_device : (i + 1) * per_device, :] = block[k * per_device : (k + 1) * per_device, :]


def stat_kernel(count, qx_ref, qy_ref, *refs):
    key_ref, query_ref, kx_ref, ky_ref, sums_ref = refs[count:]
    gather_keys(refs[:count], (kx_ref, ky_ref))
    keys, lanes = kx_ref.shape[0], lanes_of(qx_ref.shape[0])
    query_ref[...] = jnp.zeros_like(query_ref)

    def part(base, size):
        for start in range(0, qx_ref.shape[0], lanes):
            span = slice(start, start + lanes)
            x = products(kx_ref[pl.ds(base, size), :], qx_ref[span, :])
            y = products(ky_ref[pl.ds(base, size), :], qy_ref[span, :])
            query = [[0.0] * (lanes // 128) for _ in range(4)]
            for strip, columns in tiles(size, lanes):
                key = [[0.0] * 2 for _ in range(4)]
                for i, column in enumerate(columns):
                    for j, at in enumerate(column):
                        a, b = affinity(x[at]), affinity(y[at])
                        for k, value in enumerate((a, b, a * a, a * b)):
                            key[k][j] = key[k][j] + value
                            query[k][i] = query[k][i] + value
                for k in range(4):
                    for j in range(2):
                        rows = pl.ds(base + strip + 8 * j, 8)
                        if start:
                            sums_ref[k, rows, :] += key[k][j]
                        else:
                            sums_ref[k, rows, :] = key[k][j]
            for k in range(4):
                for i, value in enumerate(query[k]):
                    at = slice(start + i * 128, start + i * 128 + 128)
                    query_ref[k : k + 1, at] += jnp.sum(value, axis=0, keepdims=True)

    each_part(keys, part)
    for k in range(4):
        for row in range(0, keys, 128):
            at = slice(row, row + 128)
            key_ref[k : k + 1, at] = jnp.sum(sums_ref[k, at, :].T, axis=0, keepdims=True)


def factors(sums, scale):
    render, target, square, cross = (sums[k : k + 1, :] for k in range(4))
    by_render, by_target = scale / render, scale / target
    mix = (square * by_render * by_render - cross * by_render * by_target) / scale
    return by_render * by_render, by_render * by_target, by_render * mix


def reorder(values, size, flip):
    blocks = values.shape[1] // size
    return jnp.concatenate(
        [values[:, (i ^ flip) * size : ((i ^ flip) + 1) * size] for i in range(blocks)], axis=1
    )


def sum_pair_kernel(size, own_ref, other_ref, out_ref):
    out_ref[...] = own_ref[...] + reorder(other_ref[...], size, 1)


def grad_kernel(count, parts, scale, qx_ref, qy_ref, *refs):
    blocks, refs = refs[:count], refs[count:]
    key_sums, query_sums = refs[:count], refs[count : count + parts]
    outs = refs[count + parts : 2 * count + parts]
    kx_ref, ky_ref, key_ref, query_ref, total_ref = refs[2 * count + parts :]
    per_device = blocks[0].shape[0] // 2
    gather_keys(blocks, (kx_ref, ky_ref))

    sums = query_sums[0][...]
    for k in range(1, parts):
        sums = sums + reorder(query_sums[k][...], 2 * per_device, k)
    for k, row in enumerate(factors(sums, scale)):
        query_ref[k : k + 1, :] = row
    sums = key_sums[0][...]
    for k in range(1, count):
        sums = sums + reorder(key_sums[k][...], per_device, k)
    for k, row in enumerate(factors(sums, scale)):
        key_ref[k] = jnp.broadcast_to(row, (128, row.shape[1])).T

    lanes = lanes_of(qx_ref.shape[0])

    def part(base, size):
        rows = pl.ds(base, size)
        for start in range(0, qx_ref.shape[0], lanes):
            span = slice(start, start + lanes)
            queries = qx_ref[span, :]
            x = products(kx_ref[rows, :], queries)
            y = products(ky_ref[rows, :], qy_ref[span, :])
            query = [
                [jnp.broadcast_to(query_ref[k : k + 1, i : i + 128], (8, 128)) for k in range(3)]
                for i in range(start, start + lanes, 128)
            ]
            weights = []
            for strip, columns in tiles(size, lanes):
                row = []
                for i, column in enumerate(columns):
                    pair = []
                    for j, at in enumerate(column):
                        a, b = affinity(x[at]), affinity(y[at])
                        group = pl.ds(base + strip + 8 * j, 8)
                        square, cross, single = (key_ref[k, group, :] + query[i][k] for k in range(3))
                        pair.append(a * (a * square - b * cross - single))
                    row.append(jnp.concatenate(pair, axis=0).astype(BF16))
                weights.append(jnp.concatenate(row, axis=1))
            share = jnp.dot(
                jnp.concatenate(weights, axis=0), queries, preferred_element_type=F32
            )
            if start:
                total_ref[rows, :] += share
            else:
                total_ref[rows, :] = share

    each_part(kx_ref.shape[0], part)
    for k, out in enumerate(outs):
        out[...] = total_ref[k * per_device : (k + 1) * per_device, :].astype(out.dtype)


def last_kernel(unit_ref, norm_ref, *refs):
    parts, out_ref = refs[:-1], refs[-1]
    gradient = parts[0][...]
    for part in parts[1:]:
        gradient = gradient + part[...].astype(F32)
    unit = unit_ref[0 : gradient.shape[0], :].astype(F32)
    along = jnp.sum(unit * gradient, axis=1, keepdims=True)
    out_ref[...] = (gradient - unit * along) / norm_ref[:, :1]


def call(kernel, out_shape, args, in_specs=None, scratch=(), mib=16, flops=0, nbytes=0):
    many = isinstance(out_shape, (tuple, list))
    return pl.pallas_call(
        kernel,
        out_shape=out_shape,
        in_specs=in_specs or [VMEM] * len(args),
        out_specs=[VMEM] * len(out_shape) if many else VMEM,
        scratch_shapes=scratch,
        compiler_params=params(mib),
        cost_estimate=pl.CostEstimate(flops=flops, bytes_accessed=nbytes, transcendentals=0),
    )(*args)


def body(ray_feat, ray_pos, target_index, target_map):
    per_device, channels = ray_feat.shape
    col_count = lax.axis_size("col")
    row_count = lax.axis_size("row")
    shape = jax.ShapeDtypeStruct
    queries, keys = col_count * per_device, row_count * per_device

    def flip(values, axis, bits):
        pairs = [(i, i ^ bits) for i in range(lax.axis_size(axis))]
        return lax.ppermute(values, axis, pairs)

    me = lax.axis_index("col").astype(jnp.int32).reshape(1)
    sent = call(
        functools.partial(send_kernel, col_count),
        shape((per_device + EXTRA, channels), BF16),
        (
            lax.axis_index("row").astype(jnp.int32).reshape(1),
            ray_feat,
            ray_pos.reshape(1, -1),
            target_index.reshape(1, -1),
        ),
        in_specs=[SMEM, HBM, HBM, HBM],
        scratch=[pltpu.VMEM((1, per_device), jnp.int32)] * 2 + [pltpu.SemaphoreType.DMA((3,))],
        mib=FULL,
    )
    own_target = call(
        own_target_kernel,
        shape((per_device, channels), BF16),
        (target_index, target_map),
        in_specs=[SMEM, HBM],
        scratch=table_scratch(target_map, per_device),
        mib=24,
        nbytes=target_map.size * 2,
    )
    blocks = [sent, flip(sent, "col", 1)]
    for k in range(2, col_count, 2):
        block, own_target = lax.optimization_barrier((flip(sent, "col", k), own_target))
        blocks += [block, flip(block, "col", 1)]
    query_unit, targets, own_block, own_norm = call(
        functools.partial(pick_kernel, col_count),
        (
            shape((queries, channels), BF16),
            shape((1, col_count * channels), jnp.int32),
            shape((2 * per_device, channels), BF16),
            shape((per_device, 128), F32),
        ),
        (me, own_target, *blocks),
        in_specs=[SMEM] + [VMEM] * (col_count + 1),
        nbytes=queries * channels * 4,
    )
    key_blocks = [own_block] + [flip(own_block, "row", k) for k in range(1, row_count)]
    query_target = call(
        functools.partial(query_target_kernel, per_device),
        shape((queries, channels), BF16),
        (targets, target_map),
        in_specs=[SMEM, HBM],
        scratch=table_scratch(target_map, queries),
        mib=24,
        nbytes=target_map.size * 2,
    )

    flops = 2 * queries * keys * channels
    key_scratch = [pltpu.VMEM((keys, channels), BF16)] * 2
    key_sums, query_sums = call(
        functools.partial(stat_kernel, row_count),
        (shape((4, keys), F32), shape((4, queries), F32)),
        (query_unit, query_target, *key_blocks),
        scratch=key_scratch + [pltpu.VMEM((4, keys, 128), F32)],
        mib=32,
        flops=2 * flops,
    )
    key_parts = [key_sums] + [flip(key_sums, "row", k) for k in range(1, row_count)]
    query_sums = call(
        functools.partial(sum_pair_kernel, per_device),
        shape((4, queries), F32),
        (query_sums, flip(query_sums, "col", 1)),
    )
    query_parts = [query_sums] + [
        flip(query_sums, "col", 2 * k) for k in range(1, col_count // 2)
    ]
    scale = float(queries * row_count) / math.sqrt(HEAT)
    partials = call(
        functools.partial(grad_kernel, row_count, len(query_parts), scale),
        [shape((per_device, channels), F32 if k == 0 else BF16) for k in range(row_count)],
        (query_unit, query_target, *key_blocks, *key_parts, *query_parts),
        scratch=key_scratch
        + [
            pltpu.VMEM((3, keys, 128), F32),
            pltpu.VMEM((3, queries), F32),
            pltpu.VMEM((keys, channels), F32),
        ],
        mib=32,
        flops=3 * flops,
    )
    partials = [partials[0]] + [flip(partials[k], "row", k) for k in range(1, row_count)]
    return call(
        last_kernel,
        shape((per_device, channels), F32),
        (own_block, own_norm, *partials),
    )


def solution(mesh):
    return jax.shard_map(
        body,
        mesh=mesh,
        in_specs=(P(("row", "col"), None), P(("row", "col")), P(("row", "col")), P()),
        out_specs=P(("row", "col"), None),
        check_vma=False,
    )
```

```python
import functools
import math

import jax
import jax.numpy as jnp
from jax import lax
from jax.experimental import pallas as pl
from jax.experimental.pallas import tpu as pltpu
from jax.sharding import PartitionSpec as P

HEAT = 0.25
EPSILON = 1e-06
EXTRA = 16
BASE_BITS = 7
BASE = 1 << BASE_BITS
F32 = jnp.float32
BF16 = jnp.bfloat16
VMEM = pl.BlockSpec(memory_space=pltpu.VMEM)
SMEM = pl.BlockSpec(memory_space=pltpu.SMEM)
HBM = pl.BlockSpec(memory_space=pltpu.HBM)
FULL = 60
PIECES = 8
KEY_ROWS = 8


def params(mib):
    return pltpu.CompilerParams(vmem_limit_bytes=mib * 2**20)


def unit_rows(values):
    as_float = values.astype(F32)
    norms = jnp.sqrt(jnp.sum(as_float * as_float, axis=1, keepdims=True) + EPSILON)
    return (as_float * (1.0 / norms)).astype(BF16), norms


def table_scratch(table, rows):
    half = table.shape[1] // 2
    return [
        pltpu.VMEM(table.shape, BF16),
        pltpu.VMEM((2 * table.shape[0], half), F32),
        pltpu.VMEM((2 * rows, half), F32),
        pltpu.SemaphoreType.DMA((PIECES,)),
    ]


def load_table(table_ref, narrow_ref, wide_ref, sems, meanwhile=lambda: None):
    size = table_ref.shape[0] // PIECES
    half = table_ref.shape[1] // 2

    def copy(i):
        rows = pl.ds(i * size, size)
        return pltpu.make_async_copy(table_ref.at[rows, :], narrow_ref.at[rows, :], sems.at[i])

    for i in range(PIECES):
        copy(i).start()
    meanwhile()
    step = math.gcd(size, 256)
    for i in range(PIECES):
        copy(i).wait()

        @pl.loop(i * (size // step), (i + 1) * (size // step))
        def _(j):
            start = pl.multiple_of(j * step, step)
            values = narrow_ref[pl.ds(start, step), :].astype(F32)
            wide_ref[pl.ds(start * 2, step, 2), :] = values[:, :half]
            wide_ref[pl.ds(start * 2 + 1, step, 2), :] = values[:, half:]


def take_rows(index, start, count, wide_ref, rows_ref):
    @pl.loop(0, count // 32)
    def _(i):
        for group in range(8):
            first = i * 32 + group * 4
            rows = [wide_ref[pl.ds(index(first + j) * 2, 2), :] for j in range(4)]
            at = pl.multiple_of(start * 2 + first * 2, 8)
            rows_ref[pl.ds(at, 8), :] = jnp.concatenate(rows, axis=0)


def unit_taken(rows_ref, out_ref):
    rows, half = out_ref.shape[0], out_ref.shape[1] // 2
    step = math.gcd(rows, 64)
    for start in range(0, rows, step):
        left = rows_ref[pl.ds(2 * start, step, 2), :]
        right = rows_ref[pl.ds(2 * start + 1, step, 2), :]
        square = jnp.sum(left * left + right * right, axis=1, keepdims=True)
        inverse = 1.0 / jnp.sqrt(square + EPSILON)
        out_ref[start : start + step, :half] = (left * inverse).astype(BF16)
        out_ref[start : start + step, half:] = (right * inverse).astype(BF16)


def own_target_kernel(index_ref, table_ref, out_ref, narrow_ref, wide_ref, rows_ref, sems):
    load_table(table_ref, narrow_ref, wide_ref, sems)
    take_rows(lambda i: index_ref[i], 0, out_ref.shape[0], wide_ref, rows_ref)
    unit_taken(rows_ref, out_ref)


def query_kernel(count, target_ref, table_ref, *refs):
    blocks = refs[:count]
    unit_ref, out_ref, narrow_ref, wide_ref, rows_ref, sems = refs[count:]
    per_device = out_ref.shape[0] // count
    stride = table_ref.shape[1]

    def meanwhile():
        for i, block in enumerate(blocks):
            unit_ref[i * per_device : (i + 1) * per_device, :] = unit_rows(block[:per_device, :])[0]

    load_table(table_ref, narrow_ref, wide_ref, sems, meanwhile)
    for i in range(count):
        start = i * stride
        take_rows(lambda j: target_ref[0, start + j], i * per_device, per_device, wide_ref, rows_ref)
    unit_taken(rows_ref, out_ref)


def send_kernel(columns, row_ref, feat_ref, pos_ref, index_ref, out_ref, pos_own, index_own, sems):
    per_device, channels = feat_ref.shape
    copies = [
        pltpu.make_async_copy(pos_ref, pos_own, sems.at[0]),
        pltpu.make_async_copy(index_ref, index_own, sems.at[1]),
        pltpu.make_async_copy(feat_ref, out_ref.at[pl.ds(0, per_device), :], sems.at[2]),
    ]
    for copy in copies:
        copy.start()
    for copy in copies[:2]:
        copy.wait()
    pos, index = pos_own[...] - row_ref[0] * (columns * per_device), index_own[...]
    cell = jnp.zeros_like(pos)
    for k in range(1, columns):
        cell = cell + (pos >= k * per_device).astype(jnp.int32)
    rows = [cell, pos - cell * per_device, index >> BASE_BITS, index & (BASE - 1)]
    digits = jnp.concatenate(rows + [jnp.zeros((EXTRA - 4, per_device), jnp.int32)], axis=0)
    pad = jnp.zeros((EXTRA, channels - per_device), jnp.int32)
    digits = jnp.concatenate([digits, pad], axis=1) if channels > per_device else digits
    out_ref[per_device : per_device + EXTRA, :] = digits.astype(F32).astype(BF16)
    copies[2].wait()


def pick_kernel(count, col_ref, *refs):
    blocks = refs[:count]
    target_ref, cell_ref, norm_ref = refs[count:]
    per_device, channels = cell_ref.shape
    me = col_ref[0]
    slot = lax.broadcasted_iota(jnp.int32, (per_device, per_device), 0)
    cell = jnp.zeros((per_device, channels), F32)
    digits = [block[per_device : per_device + EXTRA, :] for block in blocks]
    table = jnp.concatenate([d[2:4, :per_device].astype(F32) for d in digits], axis=0).astype(BF16)
    for i, block in enumerate(blocks):
        feats = block[0:per_device, :]
        column, offset = (digits[i][k : k + 1, :per_device].astype(F32).astype(jnp.int32) for k in range(2))
        at_slot = jnp.where(slot == offset, 1.0, 0.0)
        found = jnp.dot(table, at_slot.astype(BF16), preferred_element_type=F32)
        target = jnp.zeros((1, per_device), F32)
        for j in range(count):
            value = found[2 * j : 2 * j + 1, :] * BASE + found[2 * j + 1 : 2 * j + 2, :]
            target = target + jnp.where((column ^ me) == j, value, 0.0)
        target_ref[:, i * channels : i * channels + per_device] = target.astype(jnp.int32)
        chosen = jnp.where(column == me, at_slot, 0.0).astype(BF16)
        cell = cell + jnp.dot(chosen, feats, preferred_element_type=F32)
    unit, norms = unit_rows(cell.astype(BF16))
    cell_ref[...] = unit
    norm_ref[...] = jnp.broadcast_to(norms, norm_ref.shape)


def products(left, right):
    return lax.dot_general(left, right, (((1,), (1,)), ((), ())), preferred_element_type=F32)


def affinity(product):
    return jnp.exp2(product * (math.log2(math.e) / HEAT))


def lanes_of(length):
    return math.gcd(length, 512)


def each_part(length, body):
    size = length if length <= 768 else math.gcd(length, 768)
    if size == length:
        body(0, size)
    else:
        pl.loop(0, length // size)(lambda i: body(pl.multiple_of(i * size, size), size))


def tiles(rows, lanes):
    for strip in range(0, rows, 16):
        yield strip, [
            [(slice(row, row + 8), slice(lane, lane + 128)) for row in range(strip, strip + 16, 8)]
            for lane in range(0, lanes, 128)
        ]


def gather_keys(blocks, whole_ref):
    per_device = blocks[0].shape[0]
    for i, block in enumerate(blocks):
        whole_ref[i * per_device : (i + 1) * per_device, :] = block[...]


def stat_kernel(count, qx_ref, qy_ref, *refs):
    key_ref, query_ref, kx_ref, ky_ref, sums_ref = refs[2 * count :]
    gather_keys(refs[:count], kx_ref)
    gather_keys(refs[count : 2 * count], ky_ref)
    keys, lanes = kx_ref.shape[0], lanes_of(qx_ref.shape[0])
    query_ref[...] = jnp.zeros_like(query_ref)

    def part(base, size):
        for start in range(0, qx_ref.shape[0], lanes):
            span = slice(start, start + lanes)
            x = products(kx_ref[pl.ds(base, size), :], qx_ref[span, :])
            y = products(ky_ref[pl.ds(base, size), :], qy_ref[span, :])
            query = [[0.0] * (lanes // 128) for _ in range(4)]
            for strip, columns in tiles(size, lanes):
                key = [[0.0] * 2 for _ in range(4)]
                for i, column in enumerate(columns):
                    for j, at in enumerate(column):
                        a, b = affinity(x[at]), affinity(y[at])
                        for k, value in enumerate((a, b, a * a, a * b)):
                            key[k][j] = key[k][j] + value
                            query[k][i] = query[k][i] + value
                for k in range(4):
                    for j in range(2):
                        rows = pl.ds(base + strip + 8 * j, 8)
                        if start:
                            sums_ref[k, rows, :] += key[k][j]
                        else:
                            sums_ref[k, rows, :] = key[k][j]
            for k in range(4):
                for i, value in enumerate(query[k]):
                    at = slice(start + i * 128, start + i * 128 + 128)
                    query_ref[k : k + 1, at] += jnp.sum(value, axis=0, keepdims=True)

    each_part(keys, part)
    key_ref[4:, :] = jnp.zeros_like(key_ref[4:, :])
    for k in range(4):
        for row in range(0, keys, 128):
            at = slice(row, row + 128)
            key_ref[k : k + 1, at] = jnp.sum(sums_ref[k, at, :].T, axis=0, keepdims=True)


def factors(sums, scale):
    render, target, square, cross = (sums[k : k + 1, :] for k in range(4))
    by_render, by_target = scale / render, scale / target
    mix = (square * by_render * by_render - cross * by_render * by_target) / scale
    return by_render * by_render, by_render * by_target, by_render * mix


def reorder(values, size, flip):
    blocks = values.shape[1] // size
    return jnp.concatenate(
        [values[:, (i ^ flip) * size : ((i ^ flip) + 1) * size] for i in range(blocks)], axis=1
    )


def sum_kernel(size, flip, own_ref, other_ref, out_ref):
    out_ref[...] = own_ref[...] + reorder(other_ref[...], size, flip)


def grad_kernel(count, chosen, rows, parts, scale, qx_ref, qy_ref, *refs):
    kx_blocks, ky_blocks, refs = refs[:count], refs[count : 2 * count], refs[2 * count :]
    key_sums, query_sums, refs = refs[:rows], refs[rows : rows + parts], refs[rows + parts :]
    outs = refs[:count]
    kx_ref, ky_ref, key_ref, query_ref, total_ref = refs[count:]
    per_device = kx_blocks[0].shape[0]
    gather_keys(kx_blocks, kx_ref)
    gather_keys(ky_blocks, ky_ref)
    sums = query_sums[0][...]
    for k in range(1, parts):
        sums = sums + reorder(query_sums[k][...], 2 * per_device, k)
    for k, row in enumerate(factors(sums, scale)):
        query_ref[k : k + 1, :] = row
    sums = key_sums[0][0:4, :]
    for k in range(1, rows):
        sums = sums + reorder(key_sums[k][0:4, :], per_device, k)
    wanted = sums[:, chosen * per_device : (chosen + count) * per_device]
    for k, row in enumerate(factors(wanted, scale)):
        key_ref[k] = jnp.broadcast_to(row, (128, row.shape[1])).T

    lanes = lanes_of(qx_ref.shape[0])

    def part(base, size):
        rows = pl.ds(base, size)
        for start in range(0, qx_ref.shape[0], lanes):
            span = slice(start, start + lanes)
            queries = qx_ref[span, :]
            x = products(kx_ref[rows, :], queries)
            y = products(ky_ref[rows, :], qy_ref[span, :])
            query = [
                [jnp.broadcast_to(query_ref[k : k + 1, i : i + 128], (8, 128)) for k in range(3)]
                for i in range(start, start + lanes, 128)
            ]
            weights = []
            for strip, columns in tiles(size, lanes):
                row = []
                for i, column in enumerate(columns):
                    pair = []
                    for j, at in enumerate(column):
                        a, b = affinity(x[at]), affinity(y[at])
                        group = pl.ds(base + strip + 8 * j, 8)
                        square, cross, single = (key_ref[k, group, :] + query[i][k] for k in range(3))
                        pair.append(a * (a * square - b * cross - single))
                    row.append(jnp.concatenate(pair, axis=0).astype(BF16))
                weights.append(jnp.concatenate(row, axis=1))
            share = jnp.dot(
                jnp.concatenate(weights, axis=0), queries, preferred_element_type=F32
            )
            if start:
                total_ref[rows, :] += share
            else:
                total_ref[rows, :] = share

    each_part(kx_ref.shape[0], part)
    for k, out in enumerate(outs):
        out[...] = total_ref[k * per_device : (k + 1) * per_device, :].astype(out.dtype)


def last_kernel(unit_ref, norm_ref, *refs):
    parts, out_ref = refs[:-1], refs[-1]
    gradient = parts[0][...]
    for part in parts[1:]:
        gradient = gradient + part[...].astype(F32)
    unit = unit_ref[...].astype(F32)
    along = jnp.sum(unit * gradient, axis=1, keepdims=True)
    out_ref[...] = (gradient - unit * along) / norm_ref[:, :1]


def call(kernel, out_shape, args, in_specs=None, scratch=(), mib=16, flops=0, nbytes=0):
    many = isinstance(out_shape, (tuple, list))
    return pl.pallas_call(
        kernel,
        out_shape=out_shape,
        in_specs=in_specs or [VMEM] * len(args),
        out_specs=[VMEM] * len(out_shape) if many else VMEM,
        scratch_shapes=scratch,
        compiler_params=params(mib),
        cost_estimate=pl.CostEstimate(flops=flops, bytes_accessed=nbytes, transcendentals=0),
    )(*args)


def body(ray_feat, ray_pos, target_index, target_map):
    per_device, channels = ray_feat.shape
    col_count = lax.axis_size("col")
    row_count = lax.axis_size("row")
    shape = jax.ShapeDtypeStruct
    queries, keys = col_count * per_device, row_count * per_device

    def flip(values, axis, bits):
        pairs = [(i, i ^ bits) for i in range(lax.axis_size(axis))]
        return lax.ppermute(values, axis, pairs)

    me = lax.axis_index("col").astype(jnp.int32).reshape(1)
    sent = call(
        functools.partial(send_kernel, col_count),
        shape((per_device + EXTRA, channels), BF16),
        (
            lax.axis_index("row").astype(jnp.int32).reshape(1),
            ray_feat,
            ray_pos.reshape(1, -1),
            target_index.reshape(1, -1),
        ),
        in_specs=[SMEM, HBM, HBM, HBM],
        scratch=[pltpu.VMEM((1, per_device), jnp.int32)] * 2 + [pltpu.SemaphoreType.DMA((3,))],
        mib=FULL,
    )
    own_target = call(
        own_target_kernel,
        shape((per_device, channels), BF16),
        (target_index, target_map),
        in_specs=[SMEM, HBM],
        scratch=table_scratch(target_map, per_device),
        mib=FULL - 8,
        nbytes=target_map.size * 2,
    )
    key_targets = [own_target] + [flip(own_target, "row", k) for k in range(1, row_count)]
    blocks = [sent, flip(sent, "col", 1)]
    for k in range(2, col_count, 2):
        block, own_target = lax.optimization_barrier((flip(sent, "col", k), own_target))
        if k == 2:
            for j in (1,2):
                block, key_targets[j] = lax.optimization_barrier((block, key_targets[j]))
        blocks += [block, flip(block, "col", 1)]
    targets, own_unit, own_norm = call(
        functools.partial(pick_kernel, col_count),
        (
            shape((1, col_count * channels), jnp.int32),
            shape((per_device, channels), BF16),
            shape((per_device, 128), F32),
        ),
        (me, *blocks),
        in_specs=[SMEM] + [VMEM] * col_count,
        nbytes=queries * channels * 4,
    )
    key_units = [own_unit] + [flip(own_unit, "row", k) for k in range(1, row_count)]
    query_unit, query_target = call(
        functools.partial(query_kernel, col_count),
        [shape((queries, channels), BF16)] * 2,
        (targets, target_map, *blocks),
        in_specs=[SMEM, HBM] + [VMEM] * col_count,
        scratch=table_scratch(target_map, queries),
        mib=FULL - 10,
        nbytes=target_map.size * 2,
    )

    flops = 2 * queries * keys * channels
    key_scratch = [pltpu.VMEM((keys, channels), BF16)] * 2
    key_sums, query_sums = call(
        functools.partial(stat_kernel, row_count),
        (shape((KEY_ROWS, keys), F32), shape((4, queries), F32)),
        (query_unit, query_target, *key_units, *key_targets),
        scratch=key_scratch + [pltpu.VMEM((4, keys, 128), F32)],
        mib=32,
        flops=2 * flops,
    )
    for k in range(max(col_count, row_count).bit_length() - 1):
        if 1 << k < row_count:
            key_sums = call(
                functools.partial(sum_kernel, per_device, 1 << k),
                shape((KEY_ROWS, keys), F32),
                (key_sums, flip(key_sums, "row", 1 << k)),
            )
        if 1 << k < col_count:
            query_sums = call(
                functools.partial(sum_kernel, per_device, 1 << k),
                shape((4, queries), F32),
                (query_sums, flip(query_sums, "col", 1 << k)),
            )
    key_parts, query_parts = [key_sums], [query_sums]
    scale = float(queries * row_count) / math.sqrt(HEAT)

    def gradient(chosen, count, dtype, query_unit):
        return call(
            functools.partial(grad_kernel, count, chosen, 1, 1, scale),
            [shape((per_device, channels), dtype)] * count,
            (
                query_unit,
                query_target,
                *key_units[chosen : chosen + count],
                *key_targets[chosen : chosen + count],
                *key_parts,
                *query_parts,
            ),
            scratch=[pltpu.VMEM((count * per_device, channels), BF16)] * 2
            + [
                pltpu.VMEM((3, count * per_device, 128), F32),
                pltpu.VMEM((3, queries), F32),
                pltpu.VMEM((count * per_device, channels), F32),
            ],
            mib=32,
            flops=3 * flops * count // row_count,
        )

    partials, query_unit = lax.optimization_barrier(
        (gradient(1, row_count - 1, BF16, query_unit), query_unit)
    )
    (own_part,) = gradient(0, 1, F32, query_unit)
    partials = [own_part] + [flip(part, "row", k + 1) for k, part in enumerate(partials)]
    return call(
        last_kernel,
        shape((per_device, channels), F32),
        (own_unit, own_norm, *partials),
    )


def solution(mesh):
    return jax.shard_map(
        body,
        mesh=mesh,
        in_specs=(P(("row", "col"), None), P(("row", "col")), P(("row", "col")), P()),
        out_specs=P(("row", "col"), None),
        check_vma=False,
    )
```

```python
import functools
import math

import jax
import jax.numpy as jnp
from jax import lax
from jax.experimental import pallas as pl
from jax.experimental.pallas import tpu as pltpu
from jax.sharding import PartitionSpec as P

HEAT = 0.25
EPSILON = 1e-06
EXTRA = 16
BASE_BITS = 7
BASE = 1 << BASE_BITS
F32 = jnp.float32
BF16 = jnp.bfloat16
VMEM = pl.BlockSpec(memory_space=pltpu.VMEM)
SMEM = pl.BlockSpec(memory_space=pltpu.SMEM)
HBM = pl.BlockSpec(memory_space=pltpu.HBM)
FULL = 60
PIECES = 8
KEY_ROWS = 8


def params(mib):
    return pltpu.CompilerParams(vmem_limit_bytes=mib * 2**20)


def unit_rows(values):
    as_float = values.astype(F32)
    norms = jnp.sqrt(jnp.sum(as_float * as_float, axis=1, keepdims=True) + EPSILON)
    return (as_float * (1.0 / norms)).astype(BF16), norms


def table_scratch(table, rows):
    half = table.shape[1] // 2
    return [
        pltpu.VMEM(table.shape, BF16),
        pltpu.VMEM((2 * table.shape[0], half), F32),
        pltpu.VMEM((2 * rows, half), F32),
        pltpu.SemaphoreType.DMA((PIECES,)),
    ]


def index_scratch(length):
    return [pltpu.SMEM((1, length), jnp.int32), pltpu.SemaphoreType.DMA(())]


def load_table(table_ref, narrow_ref, wide_ref, sems, meanwhile=lambda: None):
    size = table_ref.shape[0] // PIECES
    half = table_ref.shape[1] // 2

    def copy(i):
        rows = pl.ds(i * size, size)
        return pltpu.make_async_copy(table_ref.at[rows, :], narrow_ref.at[rows, :], sems.at[i])

    for i in range(PIECES):
        copy(i).start()
    meanwhile()
    step = math.gcd(size, 256)
    for i in range(PIECES):
        copy(i).wait()

        @pl.loop(i * (size // step), (i + 1) * (size // step))
        def _(j):
            start = pl.multiple_of(j * step, step)
            values = narrow_ref[pl.ds(start, step), :].astype(F32)
            wide_ref[pl.ds(start * 2, step, 2), :] = values[:, :half]
            wide_ref[pl.ds(start * 2 + 1, step, 2), :] = values[:, half:]


def take_rows(index, start, count, wide_ref, rows_ref):
    @pl.loop(0, count // 32)
    def _(i):
        for group in range(8):
            first = i * 32 + group * 4
            rows = [wide_ref[pl.ds(index(first + j) * 2, 2), :] for j in range(4)]
            at = pl.multiple_of(start * 2 + first * 2, 8)
            rows_ref[pl.ds(at, 8), :] = jnp.concatenate(rows, axis=0)


def unit_taken(rows_ref, out_ref):
    rows, half = out_ref.shape[0], out_ref.shape[1] // 2
    step = math.gcd(rows, 64)
    for start in range(0, rows, step):
        left = rows_ref[pl.ds(2 * start, step, 2), :]
        right = rows_ref[pl.ds(2 * start + 1, step, 2), :]
        square = jnp.sum(left * left + right * right, axis=1, keepdims=True)
        inverse = 1.0 / jnp.sqrt(square + EPSILON)
        out_ref[start : start + step, :half] = (left * inverse).astype(BF16)
        out_ref[start : start + step, half:] = (right * inverse).astype(BF16)


def own_target_kernel(list_ref, table_ref, out_ref, narrow_ref, wide_ref, rows_ref, sems, index_ref, sem):
    copy = pltpu.make_async_copy(list_ref, index_ref, sem)
    copy.start()
    load_table(table_ref, narrow_ref, wide_ref, sems)
    copy.wait()
    take_rows(lambda i: index_ref[0, i], 0, out_ref.shape[0], wide_ref, rows_ref)
    unit_taken(rows_ref, out_ref)


def query_kernel(count, list_ref, table_ref, *refs):
    blocks = refs[:count]
    unit_ref, out_ref, narrow_ref, wide_ref, rows_ref, sems, target_ref, sem = refs[count:]
    per_device = out_ref.shape[0] // count
    stride = table_ref.shape[1]

    def meanwhile():
        for i, block in enumerate(blocks):
            unit_ref[i * per_device : (i + 1) * per_device, :] = unit_rows(block[:per_device, :])[0]

    copy = pltpu.make_async_copy(list_ref, target_ref, sem)
    copy.start()
    load_table(table_ref, narrow_ref, wide_ref, sems, meanwhile)
    copy.wait()
    for i in range(count):
        start = i * stride
        take_rows(lambda j: target_ref[0, start + j], i * per_device, per_device, wide_ref, rows_ref)
    unit_taken(rows_ref, out_ref)


def send_kernel(columns, row_ref, feat_ref, pos_ref, index_ref, out_ref, list_ref, pos_own, index_own, sems):
    per_device, channels = feat_ref.shape
    copies = [
        pltpu.make_async_copy(pos_ref, pos_own, sems.at[0]),
        pltpu.make_async_copy(index_ref, index_own, sems.at[1]),
        pltpu.make_async_copy(feat_ref, out_ref.at[pl.ds(0, per_device), :], sems.at[2]),
    ]
    for copy in copies:
        copy.start()
    for copy in copies[:2]:
        copy.wait()
    pos, index = pos_own[...] - row_ref[0] * (columns * per_device), index_own[...]
    cell = jnp.zeros_like(pos)
    for k in range(1, columns):
        cell = cell + (pos >= k * per_device).astype(jnp.int32)
    list_ref[...] = jnp.zeros_like(list_ref)
    list_ref[:, :per_device] = index
    rows = [cell, pos - cell * per_device, index >> BASE_BITS, index & (BASE - 1)]
    digits = jnp.concatenate(rows + [jnp.zeros((EXTRA - 4, per_device), jnp.int32)], axis=0)
    pad = jnp.zeros((EXTRA, channels - per_device), jnp.int32)
    digits = jnp.concatenate([digits, pad], axis=1) if channels > per_device else digits
    out_ref[per_device : per_device + EXTRA, :] = digits.astype(F32).astype(BF16)
    copies[2].wait()


def pick_kernel(count, col_ref, *refs):
    blocks = refs[:count]
    target_ref, cell_ref, norm_ref = refs[count:]
    per_device, channels = cell_ref.shape
    me = col_ref[0]
    slot = lax.broadcasted_iota(jnp.int32, (per_device, per_device), 0)
    target_ref[...] = jnp.zeros_like(target_ref)
    cell = jnp.zeros((per_device, channels), F32)
    digits = [block[per_device : per_device + EXTRA, :] for block in blocks]
    table = jnp.concatenate([d[2:4, :per_device].astype(F32) for d in digits], axis=0).astype(BF16)
    for i, block in enumerate(blocks):
        feats = block[0:per_device, :]
        column, offset = (digits[i][k : k + 1, :per_device].astype(F32).astype(jnp.int32) for k in range(2))
        at_slot = jnp.where(slot == offset, 1.0, 0.0)
        found = jnp.dot(table, at_slot.astype(BF16), preferred_element_type=F32)
        target = jnp.zeros((1, per_device), F32)
        for j in range(count):
            value = found[2 * j : 2 * j + 1, :] * BASE + found[2 * j + 1 : 2 * j + 2, :]
            target = target + jnp.where((column ^ me) == j, value, 0.0)
        target_ref[:, i * channels : i * channels + per_device] = target.astype(jnp.int32)
        chosen = jnp.where(column == me, at_slot, 0.0).astype(BF16)
        cell = cell + jnp.dot(chosen, feats, preferred_element_type=F32)
    unit, norms = unit_rows(cell.astype(BF16))
    cell_ref[...] = unit
    norm_ref[...] = jnp.broadcast_to(norms, norm_ref.shape)


def products(left, right):
    return lax.dot_general(left, right, (((1,), (1,)), ((), ())), preferred_element_type=F32)


def affinity(product):
    return jnp.exp2(product * (math.log2(math.e) / HEAT))


def lanes_of(length):
    return math.gcd(length, 512)


def each_part(length, body):
    size = length if length <= 768 else math.gcd(length, 768)
    if size == length:
        body(0, size)
    else:
        pl.loop(0, length // size)(lambda i: body(pl.multiple_of(i * size, size), size))


def tiles(rows, lanes):
    for strip in range(0, rows, 16):
        yield strip, [
            [(slice(row, row + 8), slice(lane, lane + 128)) for row in range(strip, strip + 16, 8)]
            for lane in range(0, lanes, 128)
        ]


def gather_keys(blocks, whole_ref):
    per_device = blocks[0].shape[0]
    for i, block in enumerate(blocks):
        whole_ref[i * per_device : (i + 1) * per_device, :] = block[...]


def stat_kernel(count, qx_ref, qy_ref, *refs):
    key_ref, query_ref, kx_ref, ky_ref, sums_ref = refs[2 * count :]
    gather_keys(refs[:count], kx_ref)
    gather_keys(refs[count : 2 * count], ky_ref)
    keys, lanes = kx_ref.shape[0], lanes_of(qx_ref.shape[0])
    query_ref[...] = jnp.zeros_like(query_ref)

    def part(base, size):
        for start in range(0, qx_ref.shape[0], lanes):
            span = slice(start, start + lanes)
            x = products(kx_ref[pl.ds(base, size), :], qx_ref[span, :])
            y = products(ky_ref[pl.ds(base, size), :], qy_ref[span, :])
            query = [[0.0] * (lanes // 128) for _ in range(4)]
            for strip, columns in tiles(size, lanes):
                key = [[0.0] * 2 for _ in range(4)]
                for i, column in enumerate(columns):
                    for j, at in enumerate(column):
                        a, b = affinity(x[at]), affinity(y[at])
                        for k, value in enumerate((a, b, a * a, a * b)):
                            key[k][j] = key[k][j] + value
                            query[k][i] = query[k][i] + value
                for k in range(4):
                    for j in range(2):
                        rows = pl.ds(base + strip + 8 * j, 8)
                        if start:
                            sums_ref[k, rows, :] += key[k][j]
                        else:
                            sums_ref[k, rows, :] = key[k][j]
            for k in range(4):
                for i, value in enumerate(query[k]):
                    at = slice(start + i * 128, start + i * 128 + 128)
                    query_ref[k : k + 1, at] += jnp.sum(value, axis=0, keepdims=True)

    each_part(keys, part)
    key_ref[4:, :] = jnp.zeros_like(key_ref[4:, :])
    for k in range(4):
        for row in range(0, keys, 128):
            at = slice(row, row + 128)
            key_ref[k : k + 1, at] = jnp.sum(sums_ref[k, at, :].T, axis=0, keepdims=True)


def factors(sums, scale):
    render, target, square, cross = (sums[k : k + 1, :] for k in range(4))
    by_render, by_target = scale / render, scale / target
    mix = (square * by_render * by_render - cross * by_render * by_target) / scale
    return by_render * by_render, by_render * by_target, by_render * mix


def reorder(values, size, flip):
    blocks = values.shape[1] // size
    return jnp.concatenate(
        [values[:, (i ^ flip) * size : ((i ^ flip) + 1) * size] for i in range(blocks)], axis=1
    )


def sum_kernel(size, flip, own_ref, other_ref, out_ref):
    out_ref[...] = own_ref[...] + reorder(other_ref[...], size, flip)


def grad_kernel(count, chosen, rows, parts, scale, qx_ref, qy_ref, *refs):
    kx_blocks, ky_blocks, refs = refs[:count], refs[count : 2 * count], refs[2 * count :]
    key_sums, query_sums, refs = refs[:rows], refs[rows : rows + parts], refs[rows + parts :]
    outs = refs[:count]
    kx_ref, ky_ref, key_ref, query_ref, total_ref = refs[count:]
    per_device = kx_blocks[0].shape[0]
    gather_keys(kx_blocks, kx_ref)
    gather_keys(ky_blocks, ky_ref)
    sums = query_sums[0][...]
    for k in range(1, parts):
        sums = sums + reorder(query_sums[k][...], 2 * per_device, k)
    for k, row in enumerate(factors(sums, scale)):
        query_ref[k : k + 1, :] = row
    sums = key_sums[0][0:4, :]
    for k in range(1, rows):
        sums = sums + reorder(key_sums[k][0:4, :], per_device, k)
    wanted = sums[:, chosen * per_device : (chosen + count) * per_device]
    for k, row in enumerate(factors(wanted, scale)):
        key_ref[k] = jnp.broadcast_to(row, (128, row.shape[1])).T

    lanes = lanes_of(qx_ref.shape[0])

    def part(base, size):
        rows = pl.ds(base, size)
        for start in range(0, qx_ref.shape[0], lanes):
            span = slice(start, start + lanes)
            queries = qx_ref[span, :]
            x = products(kx_ref[rows, :], queries)
            y = products(ky_ref[rows, :], qy_ref[span, :])
            query = [
                [jnp.broadcast_to(query_ref[k : k + 1, i : i + 128], (8, 128)) for k in range(3)]
                for i in range(start, start + lanes, 128)
            ]
            weights = []
            for strip, columns in tiles(size, lanes):
                row = []
                for i, column in enumerate(columns):
                    pair = []
                    for j, at in enumerate(column):
                        a, b = affinity(x[at]), affinity(y[at])
                        group = pl.ds(base + strip + 8 * j, 8)
                        square, cross, single = (key_ref[k, group, :] + query[i][k] for k in range(3))
                        pair.append(a * (a * square - b * cross - single))
                    row.append(jnp.concatenate(pair, axis=0).astype(BF16))
                weights.append(jnp.concatenate(row, axis=1))
            share = jnp.dot(
                jnp.concatenate(weights, axis=0), queries, preferred_element_type=F32
            )
            if start:
                total_ref[rows, :] += share
            else:
                total_ref[rows, :] = share

    each_part(kx_ref.shape[0], part)
    for k, out in enumerate(outs):
        out[...] = total_ref[k * per_device : (k + 1) * per_device, :].astype(out.dtype)


def last_kernel(unit_ref, norm_ref, *refs):
    parts, out_ref = refs[:-1], refs[-1]
    gradient = parts[0][...]
    for part in parts[1:]:
        gradient = gradient + part[...].astype(F32)
    unit = unit_ref[...].astype(F32)
    along = jnp.sum(unit * gradient, axis=1, keepdims=True)
    out_ref[...] = (gradient - unit * along) / norm_ref[:, :1]


def call(kernel, out_shape, args, in_specs=None, scratch=(), mib=16, flops=0, nbytes=0):
    many = isinstance(out_shape, (tuple, list))
    return pl.pallas_call(
        kernel,
        out_shape=out_shape,
        in_specs=in_specs or [VMEM] * len(args),
        out_specs=[VMEM] * len(out_shape) if many else VMEM,
        scratch_shapes=scratch,
        compiler_params=params(mib),
        cost_estimate=pl.CostEstimate(flops=flops, bytes_accessed=nbytes, transcendentals=0),
    )(*args)


def body(ray_feat, ray_pos, target_index, target_map):
    per_device, channels = ray_feat.shape
    col_count = lax.axis_size("col")
    row_count = lax.axis_size("row")
    shape = jax.ShapeDtypeStruct
    queries, keys = col_count * per_device, row_count * per_device

    def flip(values, axis, bits):
        pairs = [(i, i ^ bits) for i in range(lax.axis_size(axis))]
        return lax.ppermute(values, axis, pairs)

    me = lax.axis_index("col").astype(jnp.int32).reshape(1)
    sent, own_list = call(
        functools.partial(send_kernel, col_count),
        (shape((per_device + EXTRA, channels), BF16), shape((1, channels), jnp.int32)),
        (
            lax.axis_index("row").astype(jnp.int32).reshape(1),
            ray_feat,
            ray_pos.reshape(1, -1),
            target_index.reshape(1, -1),
        ),
        in_specs=[SMEM, HBM, HBM, HBM],
        scratch=[pltpu.VMEM((1, per_device), jnp.int32)] * 2 + [pltpu.SemaphoreType.DMA((3,))],
        mib=FULL,
    )
    own_target = call(
        own_target_kernel,
        shape((per_device, channels), BF16),
        (own_list, target_map),
        in_specs=[VMEM, HBM],
        scratch=table_scratch(target_map, per_device) + index_scratch(channels),
        mib=FULL - 8,
        nbytes=target_map.size * 2,
    )
    key_targets = [own_target] + [flip(own_target, "row", k) for k in range(1, row_count)]
    blocks = [sent, flip(sent, "col", 1)]
    for k in range(2, col_count, 2):
        block, own_target = lax.optimization_barrier((flip(sent, "col", k), own_target))
        if k == col_count - 2:
            for j in range(1, min(row_count, 3)):
                block, key_targets[j] = lax.optimization_barrier((block, key_targets[j]))
        blocks += [block, flip(block, "col", 1)]
    targets, own_unit, own_norm = call(
        functools.partial(pick_kernel, col_count),
        (
            shape((1, col_count * channels), jnp.int32),
            shape((per_device, channels), BF16),
            shape((per_device, 128), F32),
        ),
        (me, *blocks),
        in_specs=[SMEM] + [VMEM] * col_count,
        nbytes=queries * channels * 4,
    )
    key_units = [own_unit] + [flip(own_unit, "row", k) for k in range(1, row_count)]
    query_unit, query_target = call(
        functools.partial(query_kernel, col_count),
        [shape((queries, channels), BF16)] * 2,
        (targets, target_map, *blocks),
        in_specs=[VMEM, HBM] + [VMEM] * col_count,
        scratch=table_scratch(target_map, queries) + index_scratch(col_count * channels),
        mib=FULL - 10,
        nbytes=target_map.size * 2,
    )

    flops = 2 * queries * keys * channels
    key_scratch = [pltpu.VMEM((keys, channels), BF16)] * 2
    key_sums, query_sums = call(
        functools.partial(stat_kernel, row_count),
        (shape((KEY_ROWS, keys), F32), shape((4, queries), F32)),
        (query_unit, query_target, *key_units, *key_targets),
        scratch=key_scratch + [pltpu.VMEM((4, keys, 128), F32)],
        mib=32,
        flops=2 * flops,
    )
    for k in range(max(col_count, row_count).bit_length() - 1):
        if 1 << k < row_count:
            key_sums = call(
                functools.partial(sum_kernel, per_device, 1 << k),
                shape((KEY_ROWS, keys), F32),
                (key_sums, flip(key_sums, "row", 1 << k)),
            )
        if 1 << k < col_count:
            other = (2 << k) if (2 << k) < col_count else 1
            query_sums = call(
                functools.partial(sum_kernel, per_device, other),
                shape((4, queries), F32),
                (query_sums, flip(query_sums, "col", other)),
            )
    key_parts, query_parts = [key_sums], [query_sums]
    scale = float(queries * row_count) / math.sqrt(HEAT)

    def gradient(chosen, count, dtype, query_unit):
        return call(
            functools.partial(grad_kernel, count, chosen, 1, 1, scale),
            [shape((per_device, channels), dtype)] * count,
            (
                query_unit,
                query_target,
                *key_units[chosen : chosen + count],
                *key_targets[chosen : chosen + count],
                *key_parts,
                *query_parts,
            ),
            scratch=[pltpu.VMEM((count * per_device, channels), BF16)] * 2
            + [
                pltpu.VMEM((3, count * per_device, 128), F32),
                pltpu.VMEM((3, queries), F32),
                pltpu.VMEM((count * per_device, channels), F32),
            ],
            mib=32,
            flops=3 * flops * count // row_count,
        )

    partials, query_unit = lax.optimization_barrier(
        (gradient(1, row_count - 1, BF16, query_unit), query_unit)
    )
    (own_part,) = gradient(0, 1, F32, query_unit)
    partials = [own_part] + [flip(part, "row", k + 1) for k, part in enumerate(partials)]
    return call(
        last_kernel,
        shape((per_device, channels), F32),
        (own_unit, own_norm, *partials),
    )


def solution(mesh):
    return jax.shard_map(
        body,
        mesh=mesh,
        in_specs=(P(("row", "col"), None), P(("row", "col")), P(("row", "col")), P()),
        out_specs=P(("row", "col"), None),
        check_vma=False,
    )
```

```python
import functools
import math

import jax
import jax.numpy as jnp
from jax import lax
from jax.experimental import pallas as pl
from jax.experimental.pallas import tpu as pltpu
from jax.sharding import PartitionSpec as P

HEAT = 0.25
EPSILON = 1e-06
EXTRA = 16
BASE_BITS = 7
BASE = 1 << BASE_BITS
F32 = jnp.float32
BF16 = jnp.bfloat16
VMEM = pl.BlockSpec(memory_space=pltpu.VMEM)
SMEM = pl.BlockSpec(memory_space=pltpu.SMEM)
HBM = pl.BlockSpec(memory_space=pltpu.HBM)
FULL = 60
PIECES = 8
KEY_ROWS = 8


def params(mib):
    return pltpu.CompilerParams(vmem_limit_bytes=mib * 2**20)


def unit_rows(values):
    as_float = values.astype(F32)
    norms = jnp.sqrt(jnp.sum(as_float * as_float, axis=1, keepdims=True) + EPSILON)
    return (as_float * (1.0 / norms)).astype(BF16), norms


def table_scratch(table, rows):
    half = table.shape[1] // 2
    return [
        pltpu.VMEM(table.shape, BF16),
        pltpu.VMEM((2 * table.shape[0], half), F32),
        pltpu.VMEM((2 * rows, half), F32),
        pltpu.SemaphoreType.DMA((PIECES,)),
    ]


def index_scratch(length):
    return [pltpu.SMEM((1, length), jnp.int32), pltpu.SemaphoreType.DMA(())]


def load_table(table_ref, narrow_ref, wide_ref, sems, meanwhile=lambda: None):
    size = table_ref.shape[0] // PIECES
    half = table_ref.shape[1] // 2

    def copy(i):
        rows = pl.ds(i * size, size)
        return pltpu.make_async_copy(table_ref.at[rows, :], narrow_ref.at[rows, :], sems.at[i])

    for i in range(PIECES):
        copy(i).start()
    meanwhile()
    step = math.gcd(size, 256)
    for i in range(PIECES):
        copy(i).wait()

        @pl.loop(i * (size // step), (i + 1) * (size // step))
        def _(j):
            start = pl.multiple_of(j * step, step)
            values = narrow_ref[pl.ds(start, step), :].astype(F32)
            wide_ref[pl.ds(start * 2, step, 2), :] = values[:, :half]
            wide_ref[pl.ds(start * 2 + 1, step, 2), :] = values[:, half:]


def take_rows(index, start, count, wide_ref, rows_ref):
    @pl.loop(0, count // 32)
    def _(i):
        for group in range(8):
            first = i * 32 + group * 4
            rows = [wide_ref[pl.ds(index(first + j) * 2, 2), :] for j in range(4)]
            at = pl.multiple_of(start * 2 + first * 2, 8)
            rows_ref[pl.ds(at, 8), :] = jnp.concatenate(rows, axis=0)


def unit_taken(rows_ref, out_ref):
    rows, half = out_ref.shape[0], out_ref.shape[1] // 2
    step = math.gcd(rows, 64)
    for start in range(0, rows, step):
        left = rows_ref[pl.ds(2 * start, step, 2), :]
        right = rows_ref[pl.ds(2 * start + 1, step, 2), :]
        square = jnp.sum(left * left + right * right, axis=1, keepdims=True)
        inverse = 1.0 / jnp.sqrt(square + EPSILON)
        out_ref[start : start + step, :half] = (left * inverse).astype(BF16)
        out_ref[start : start + step, half:] = (right * inverse).astype(BF16)


def own_target_kernel(list_ref, table_ref, out_ref, narrow_ref, wide_ref, rows_ref, sems, index_ref, sem):
    copy = pltpu.make_async_copy(list_ref, index_ref, sem)
    copy.start()
    load_table(table_ref, narrow_ref, wide_ref, sems)
    copy.wait()
    take_rows(lambda i: index_ref[0, i], 0, out_ref.shape[0], wide_ref, rows_ref)
    unit_taken(rows_ref, out_ref)


def query_kernel(count, list_ref, table_ref, *refs):
    blocks = refs[:count]
    unit_ref, out_ref, narrow_ref, wide_ref, rows_ref, sems, target_ref, sem = refs[count:]
    per_device = out_ref.shape[0] // count
    stride = table_ref.shape[1]

    def meanwhile():
        for i, block in enumerate(blocks):
            unit_ref[i * per_device : (i + 1) * per_device, :] = unit_rows(block[:per_device, :])[0]

    copy = pltpu.make_async_copy(list_ref, target_ref, sem)
    copy.start()
    load_table(table_ref, narrow_ref, wide_ref, sems, meanwhile)
    copy.wait()
    for i in range(count):
        start = i * stride
        take_rows(lambda j: target_ref[0, start + j], i * per_device, per_device, wide_ref, rows_ref)
    unit_taken(rows_ref, out_ref)


def send_kernel(columns, row_ref, feat_ref, pos_ref, index_ref, out_ref, list_ref, pos_own, index_own, sems):
    per_device, channels = feat_ref.shape
    copies = [
        pltpu.make_async_copy(pos_ref, pos_own, sems.at[0]),
        pltpu.make_async_copy(index_ref, index_own, sems.at[1]),
        pltpu.make_async_copy(feat_ref, out_ref.at[pl.ds(0, per_device), :], sems.at[2]),
    ]
    for copy in copies:
        copy.start()
    for copy in copies[:2]:
        copy.wait()
    pos, index = pos_own[...] - row_ref[0] * (columns * per_device), index_own[...]
    cell = jnp.zeros_like(pos)
    for k in range(1, columns):
        cell = cell + (pos >= k * per_device).astype(jnp.int32)
    list_ref[...] = jnp.zeros_like(list_ref)
    list_ref[:, :per_device] = index
    rows = [cell, pos - cell * per_device, index >> BASE_BITS, index & (BASE - 1)]
    digits = jnp.concatenate(rows + [jnp.zeros((EXTRA - 4, per_device), jnp.int32)], axis=0)
    pad = jnp.zeros((EXTRA, channels - per_device), jnp.int32)
    digits = jnp.concatenate([digits, pad], axis=1) if channels > per_device else digits
    out_ref[per_device : per_device + EXTRA, :] = digits.astype(F32).astype(BF16)
    copies[2].wait()


def pick_kernel(count, col_ref, *refs):
    blocks = refs[:count]
    target_ref, cell_ref, norm_ref = refs[count:]
    per_device, channels = cell_ref.shape
    me = col_ref[0]
    slot = lax.broadcasted_iota(jnp.int32, (per_device, per_device), 0)
    target_ref[...] = jnp.zeros_like(target_ref)
    cell = jnp.zeros((per_device, channels), F32)
    digits = [block[per_device : per_device + EXTRA, :] for block in blocks]
    table = jnp.concatenate([d[2:4, :per_device].astype(F32) for d in digits], axis=0).astype(BF16)
    for i, block in enumerate(blocks):
        feats = block[0:per_device, :]
        column, offset = (digits[i][k : k + 1, :per_device].astype(F32).astype(jnp.int32) for k in range(2))
        at_slot = jnp.where(slot == offset, 1.0, 0.0)
        found = jnp.dot(table, at_slot.astype(BF16), preferred_element_type=F32)
        target = jnp.zeros((1, per_device), F32)
        for j in range(count):
            value = found[2 * j : 2 * j + 1, :] * BASE + found[2 * j + 1 : 2 * j + 2, :]
            target = target + jnp.where((column ^ me) == j, value, 0.0)
        target_ref[:, i * channels : i * channels + per_device] = target.astype(jnp.int32)
        chosen = jnp.where(column == me, at_slot, 0.0).astype(BF16)
        cell = cell + jnp.dot(chosen, feats, preferred_element_type=F32)
    unit, norms = unit_rows(cell.astype(BF16))
    cell_ref[...] = unit
    norm_ref[...] = jnp.broadcast_to(norms, norm_ref.shape)


def products(left, right):
    return lax.dot_general(left, right, (((1,), (1,)), ((), ())), preferred_element_type=F32)


def affinity(product):
    return jnp.exp2(product * (math.log2(math.e) / HEAT))


def lanes_of(length):
    return math.gcd(length, 512)


def each_part(length, body):
    size = length if length <= 768 else math.gcd(length, 768)
    if size == length:
        body(0, size)
    else:
        pl.loop(0, length // size)(lambda i: body(pl.multiple_of(i * size, size), size))


def tiles(rows, lanes):
    for strip in range(0, rows, 16):
        yield strip, [
            [(slice(row, row + 8), slice(lane, lane + 128)) for row in range(strip, strip + 16, 8)]
            for lane in range(0, lanes, 128)
        ]


def gather_keys(blocks, whole_ref):
    per_device = blocks[0].shape[0]
    for i, block in enumerate(blocks):
        whole_ref[i * per_device : (i + 1) * per_device, :] = block[...]


def stat_kernel(count, qx_ref, qy_ref, *refs):
    key_ref, query_ref, kx_ref, ky_ref, sums_ref = refs[2 * count :]
    gather_keys(refs[:count], kx_ref)
    gather_keys(refs[count : 2 * count], ky_ref)
    keys, lanes = kx_ref.shape[0], lanes_of(qx_ref.shape[0])
    query_ref[...] = jnp.zeros_like(query_ref)

    def part(base, size):
        for start in range(0, qx_ref.shape[0], lanes):
            span = slice(start, start + lanes)
            x = products(kx_ref[pl.ds(base, size), :], qx_ref[span, :])
            y = products(ky_ref[pl.ds(base, size), :], qy_ref[span, :])
            query = [[0.0] * (lanes // 128) for _ in range(4)]
            for strip, columns in tiles(size, lanes):
                key = [[0.0] * 2 for _ in range(4)]
                for i, column in enumerate(columns):
                    for j, at in enumerate(column):
                        a, b = affinity(x[at]), affinity(y[at])
                        for k, value in enumerate((a, b, a * a, a * b)):
                            key[k][j] = key[k][j] + value
                            query[k][i] = query[k][i] + value
                for k in range(4):
                    for j in range(2):
                        rows = pl.ds(base + strip + 8 * j, 8)
                        if start:
                            sums_ref[k, rows, :] += key[k][j]
                        else:
                            sums_ref[k, rows, :] = key[k][j]
            for k in range(4):
                for i, value in enumerate(query[k]):
                    at = slice(start + i * 128, start + i * 128 + 128)
                    query_ref[k : k + 1, at] += jnp.sum(value, axis=0, keepdims=True)

    each_part(keys, part)
    key_ref[4:, :] = jnp.zeros_like(key_ref[4:, :])
    for k in range(4):
        for row in range(0, keys, 128):
            at = slice(row, row + 128)
            key_ref[k : k + 1, at] = jnp.sum(sums_ref[k, at, :].T, axis=0, keepdims=True)


def factors(sums, scale):
    render, target, square, cross = (sums[k : k + 1, :] for k in range(4))
    by_render, by_target = scale / render, scale / target
    mix = (square * by_render * by_render - cross * by_render * by_target) / scale
    return by_render * by_render, by_render * by_target, by_render * mix


def reorder(values, size, flip):
    blocks = values.shape[1] // size
    return jnp.concatenate(
        [values[:, (i ^ flip) * size : ((i ^ flip) + 1) * size] for i in range(blocks)], axis=1
    )


def sum_kernel(size, flip, own_ref, other_ref, out_ref):
    out_ref[...] = own_ref[...] + reorder(other_ref[...], size, flip)


def grad_kernel(count, chosen, rows, parts, scale, qx_ref, qy_ref, *refs):
    kx_blocks, ky_blocks, refs = refs[:count], refs[count : 2 * count], refs[2 * count :]
    key_sums, query_sums, refs = refs[:rows], refs[rows : rows + parts], refs[rows + parts :]
    outs = refs[:count]
    kx_ref, ky_ref, key_ref, query_ref, total_ref = refs[count:]
    per_device = kx_blocks[0].shape[0]
    gather_keys(kx_blocks, kx_ref)
    gather_keys(ky_blocks, ky_ref)
    sums = query_sums[0][...]
    for k in range(1, parts):
        sums = sums + reorder(query_sums[k][...], 2 * per_device, k)
    for k, row in enumerate(factors(sums, scale)):
        query_ref[k : k + 1, :] = row
    sums = key_sums[0][0:4, :]
    for k in range(1, rows):
        sums = sums + reorder(key_sums[k][0:4, :], per_device, k)
    wanted = sums[:, chosen * per_device : (chosen + count) * per_device]
    for k, row in enumerate(factors(wanted, scale)):
        key_ref[k] = jnp.broadcast_to(row, (128, row.shape[1])).T

    lanes = lanes_of(qx_ref.shape[0])

    def part(base, size):
        rows = pl.ds(base, size)
        for start in range(0, qx_ref.shape[0], lanes):
            span = slice(start, start + lanes)
            queries = qx_ref[span, :]
            x = products(kx_ref[rows, :], queries)
            y = products(ky_ref[rows, :], qy_ref[span, :])
            query = [
                [jnp.broadcast_to(query_ref[k : k + 1, i : i + 128], (8, 128)) for k in range(3)]
                for i in range(start, start + lanes, 128)
            ]
            weights = []
            for strip, columns in tiles(size, lanes):
                row = []
                for i, column in enumerate(columns):
                    pair = []
                    for j, at in enumerate(column):
                        a, b = affinity(x[at]), affinity(y[at])
                        group = pl.ds(base + strip + 8 * j, 8)
                        square, cross, single = (key_ref[k, group, :] + query[i][k] for k in range(3))
                        pair.append(a * (a * square - b * cross - single))
                    row.append(jnp.concatenate(pair, axis=0).astype(BF16))
                weights.append(jnp.concatenate(row, axis=1))
            share = jnp.dot(
                jnp.concatenate(weights, axis=0), queries, preferred_element_type=F32
            )
            if start:
                total_ref[rows, :] += share
            else:
                total_ref[rows, :] = share

    each_part(kx_ref.shape[0], part)
    for k, out in enumerate(outs):
        out[...] = total_ref[k * per_device : (k + 1) * per_device, :].astype(out.dtype)


def last_kernel(unit_ref, norm_ref, *refs):
    parts, out_ref = refs[:-1], refs[-1]
    gradient = parts[0][...]
    for part in parts[1:]:
        gradient = gradient + part[...].astype(F32)
    unit = unit_ref[...].astype(F32)
    along = jnp.sum(unit * gradient, axis=1, keepdims=True)
    out_ref[...] = (gradient - unit * along) / norm_ref[:, :1]


def call(kernel, out_shape, args, in_specs=None, scratch=(), mib=16, flops=0, nbytes=0):
    many = isinstance(out_shape, (tuple, list))
    return pl.pallas_call(
        kernel,
        out_shape=out_shape,
        in_specs=in_specs or [VMEM] * len(args),
        out_specs=[VMEM] * len(out_shape) if many else VMEM,
        scratch_shapes=scratch,
        compiler_params=params(mib),
        cost_estimate=pl.CostEstimate(flops=flops, bytes_accessed=nbytes, transcendentals=0),
    )(*args)


def body(ray_feat, ray_pos, target_index, target_map):
    per_device, channels = ray_feat.shape
    col_count = lax.axis_size("col")
    row_count = lax.axis_size("row")
    shape = jax.ShapeDtypeStruct
    queries, keys = col_count * per_device, row_count * per_device

    def flip(values, axis, bits):
        pairs = [(i, i ^ bits) for i in range(lax.axis_size(axis))]
        return lax.ppermute(values, axis, pairs)

    me = lax.axis_index("col").astype(jnp.int32).reshape(1)
    sent, own_list = call(
        functools.partial(send_kernel, col_count),
        (
            pltpu.VMEM((per_device + EXTRA, channels), BF16),
            pltpu.VMEM((1, channels), jnp.int32),
        ),
        (
            lax.axis_index("row").astype(jnp.int32).reshape(1),
            ray_feat,
            ray_pos.reshape(1, -1),
            target_index.reshape(1, -1),
        ),
        in_specs=[SMEM, HBM, HBM, HBM],
        scratch=[pltpu.VMEM((1, per_device), jnp.int32)] * 2 + [pltpu.SemaphoreType.DMA((3,))],
        mib=FULL,
    )
    own_target = call(
        own_target_kernel,
        shape((per_device, channels), BF16),
        (own_list, target_map),
        in_specs=[VMEM, HBM],
        scratch=table_scratch(target_map, per_device) + index_scratch(channels),
        mib=FULL - 8,
        nbytes=target_map.size * 2,
    )
    key_targets = [own_target] + [flip(own_target, "row", k) for k in range(1, row_count)]
    blocks = [sent, flip(sent, "col", 1)]
    for k in range(2, col_count, 2):
        block, own_target = lax.optimization_barrier((flip(sent, "col", k), own_target))
        if k == col_count - 2:
            for j in range(1, min(row_count, 3)):
                block, key_targets[j] = lax.optimization_barrier((block, key_targets[j]))
        blocks += [block, flip(block, "col", 1)]
    targets, own_unit, own_norm = call(
        functools.partial(pick_kernel, col_count),
        (
            shape((1, col_count * channels), jnp.int32),
            shape((per_device, channels), BF16),
            shape((per_device, 128), F32),
        ),
        (me, *blocks),
        in_specs=[SMEM] + [VMEM] * col_count,
        nbytes=queries * channels * 4,
    )
    key_units = [own_unit] + [flip(own_unit, "row", k) for k in range(1, row_count)]
    query_unit, query_target = call(
        functools.partial(query_kernel, col_count),
        [shape((queries, channels), BF16)] * 2,
        (targets, target_map, *blocks),
        in_specs=[VMEM, HBM] + [VMEM] * col_count,
        scratch=table_scratch(target_map, queries) + index_scratch(col_count * channels),
        mib=FULL - 10,
        nbytes=target_map.size * 2,
    )

    flops = 2 * queries * keys * channels
    key_scratch = [pltpu.VMEM((keys, channels), BF16)] * 2
    key_sums, query_sums = call(
        functools.partial(stat_kernel, row_count),
        (shape((KEY_ROWS, keys), F32), shape((4, queries), F32)),
        (query_unit, query_target, *key_units, *key_targets),
        scratch=key_scratch + [pltpu.VMEM((4, keys, 128), F32)],
        mib=32,
        flops=2 * flops,
    )
    for k in range(max(col_count, row_count).bit_length() - 1):
        if 1 << k < row_count:
            key_sums = call(
                functools.partial(sum_kernel, per_device, 1 << k),
                shape((KEY_ROWS, keys), F32),
                (key_sums, flip(key_sums, "row", 1 << k)),
            )
        if 1 << k < col_count:
            other = (2 << k) if (2 << k) < col_count else 1
            query_sums = call(
                functools.partial(sum_kernel, per_device, other),
                shape((4, queries), F32),
                (query_sums, flip(query_sums, "col", other)),
            )
    key_parts, query_parts = [key_sums], [query_sums]
    scale = float(queries * row_count) / math.sqrt(HEAT)

    def gradient(chosen, count, dtype, query_unit):
        return call(
            functools.partial(grad_kernel, count, chosen, 1, 1, scale),
            [shape((per_device, channels), dtype)] * count,
            (
                query_unit,
                query_target,
                *key_units[chosen : chosen + count],
                *key_targets[chosen : chosen + count],
                *key_parts,
                *query_parts,
            ),
            scratch=[pltpu.VMEM((count * per_device, channels), BF16)] * 2
            + [
                pltpu.VMEM((3, count * per_device, 128), F32),
                pltpu.VMEM((3, queries), F32),
                pltpu.VMEM((count * per_device, channels), F32),
            ],
            mib=32,
            flops=3 * flops * count // row_count,
        )

    partials, query_unit = lax.optimization_barrier(
        (gradient(1, row_count - 1, BF16, query_unit), query_unit)
    )
    (own_part,) = gradient(0, 1, F32, query_unit)
    partials = [own_part] + [flip(part, "row", k + 1) for k, part in enumerate(partials)]
    return call(
        last_kernel,
        shape((per_device, channels), F32),
        (own_unit, own_norm, *partials),
    )


def solution(mesh):
    return jax.shard_map(
        body,
        mesh=mesh,
        in_specs=(P(("row", "col"), None), P(("row", "col")), P(("row", "col")), P()),
        out_specs=P(("row", "col"), None),
        check_vma=False,
    )
```

```python
import functools
import math

import jax
import jax.numpy as jnp
from jax import lax
from jax.experimental import pallas as pl
from jax.experimental.pallas import tpu as pltpu
from jax.sharding import PartitionSpec as P

HEAT = 0.25
EPSILON = 1e-06
EXTRA = 16
BASE_BITS = 7
BASE = 1 << BASE_BITS
F32 = jnp.float32
BF16 = jnp.bfloat16
VMEM = pl.BlockSpec(memory_space=pltpu.VMEM)
SMEM = pl.BlockSpec(memory_space=pltpu.SMEM)
HBM = pl.BlockSpec(memory_space=pltpu.HBM)
FULL = 60
PIECES = 8
KEY_ROWS = 8


def params(mib):
    return pltpu.CompilerParams(vmem_limit_bytes=mib * 2**20)


def unit_rows(values):
    as_float = values.astype(F32)
    norms = jnp.sqrt(jnp.sum(as_float * as_float, axis=1, keepdims=True) + EPSILON)
    return (as_float * (1.0 / norms)).astype(BF16), norms


def table_scratch(table, rows):
    half = table.shape[1] // 2
    return [
        pltpu.VMEM(table.shape, BF16),
        pltpu.VMEM((2 * table.shape[0], half), F32),
        pltpu.VMEM((2 * rows, half), F32),
        pltpu.SemaphoreType.DMA((PIECES,)),
    ]


def index_scratch(length):
    return [pltpu.SMEM((1, length), jnp.int32), pltpu.SemaphoreType.DMA(())]


def load_table(table_ref, narrow_ref, wide_ref, sems, meanwhile=lambda: None):
    size = table_ref.shape[0] // PIECES
    half = table_ref.shape[1] // 2

    def copy(i):
        rows = pl.ds(i * size, size)
        return pltpu.make_async_copy(table_ref.at[rows, :], narrow_ref.at[rows, :], sems.at[i])

    for i in range(PIECES):
        copy(i).start()
    meanwhile()
    step = math.gcd(size, 256)
    for i in range(PIECES):
        copy(i).wait()

        @pl.loop(i * (size // step), (i + 1) * (size // step))
        def _(j):
            start = pl.multiple_of(j * step, step)
            values = narrow_ref[pl.ds(start, step), :].astype(F32)
            wide_ref[pl.ds(start * 2, step, 2), :] = values[:, :half]
            wide_ref[pl.ds(start * 2 + 1, step, 2), :] = values[:, half:]


def take_rows(index, start, count, wide_ref, rows_ref):
    @pl.loop(0, count // 32)
    def _(i):
        for group in range(8):
            first = i * 32 + group * 4
            rows = [wide_ref[pl.ds(index(first + j) * 2, 2), :] for j in range(4)]
            at = pl.multiple_of(start * 2 + first * 2, 8)
            rows_ref[pl.ds(at, 8), :] = jnp.concatenate(rows, axis=0)


def unit_taken(rows_ref, out_ref):
    rows, half = out_ref.shape[0], out_ref.shape[1] // 2
    step = math.gcd(rows, 64)
    for start in range(0, rows, step):
        left = rows_ref[pl.ds(2 * start, step, 2), :]
        right = rows_ref[pl.ds(2 * start + 1, step, 2), :]
        square = jnp.sum(left * left + right * right, axis=1, keepdims=True)
        inverse = 1.0 / jnp.sqrt(square + EPSILON)
        out_ref[start : start + step, :half] = (left * inverse).astype(BF16)
        out_ref[start : start + step, half:] = (right * inverse).astype(BF16)


def own_target_kernel(list_ref, table_ref, out_ref, narrow_ref, wide_ref, rows_ref, sems, index_ref, sem):
    copy = pltpu.make_async_copy(list_ref, index_ref, sem)
    copy.start()
    load_table(table_ref, narrow_ref, wide_ref, sems)
    copy.wait()
    take_rows(lambda i: index_ref[0, i], 0, out_ref.shape[0], wide_ref, rows_ref)
    unit_taken(rows_ref, out_ref)


def query_kernel(count, list_ref, table_ref, *refs):
    blocks = refs[:count]
    unit_ref, out_ref, narrow_ref, wide_ref, rows_ref, sems, target_ref, sem = refs[count:]
    per_device = out_ref.shape[0] // count
    stride = table_ref.shape[1]

    def meanwhile():
        for i, block in enumerate(blocks):
            unit_ref[i * per_device : (i + 1) * per_device, :] = unit_rows(block[:per_device, :])[0]

    copy = pltpu.make_async_copy(list_ref, target_ref, sem)
    copy.start()
    load_table(table_ref, narrow_ref, wide_ref, sems, meanwhile)
    copy.wait()
    for i in range(count):
        start = i * stride
        take_rows(lambda j: target_ref[0, start + j], i * per_device, per_device, wide_ref, rows_ref)
    unit_taken(rows_ref, out_ref)


def send_kernel(columns, row_ref, feat_ref, pos_ref, index_ref, out_ref, list_ref, pos_own, index_own, sems):
    per_device, channels = feat_ref.shape
    copies = [
        pltpu.make_async_copy(pos_ref, pos_own, sems.at[0]),
        pltpu.make_async_copy(index_ref, index_own, sems.at[1]),
        pltpu.make_async_copy(feat_ref, out_ref.at[pl.ds(0, per_device), :], sems.at[2]),
    ]
    for copy in copies:
        copy.start()
    for copy in copies[:2]:
        copy.wait()
    pos, index = pos_own[...] - row_ref[0] * (columns * per_device), index_own[...]
    cell = jnp.zeros_like(pos)
    for k in range(1, columns):
        cell = cell + (pos >= k * per_device).astype(jnp.int32)
    list_ref[...] = jnp.zeros_like(list_ref)
    list_ref[:, :per_device] = index
    rows = [cell, pos - cell * per_device, index >> BASE_BITS, index & (BASE - 1)]
    digits = jnp.concatenate(rows + [jnp.zeros((EXTRA - 4, per_device), jnp.int32)], axis=0)
    pad = jnp.zeros((EXTRA, channels - per_device), jnp.int32)
    digits = jnp.concatenate([digits, pad], axis=1) if channels > per_device else digits
    out_ref[per_device : per_device + EXTRA, :] = digits.astype(F32).astype(BF16)
    copies[2].wait()


def pick_kernel(count, col_ref, *refs):
    blocks = refs[:count]
    target_ref, cell_ref, norm_ref = refs[count:]
    per_device, channels = cell_ref.shape
    me = col_ref[0]
    slot = lax.broadcasted_iota(jnp.int32, (per_device, per_device), 0)
    target_ref[...] = jnp.zeros_like(target_ref)
    cell = jnp.zeros((per_device, channels), F32)
    digits = [block[per_device : per_device + EXTRA, :] for block in blocks]
    table = jnp.concatenate([d[2:4, :per_device].astype(F32) for d in digits], axis=0).astype(BF16)
    for i, block in enumerate(blocks):
        feats = block[0:per_device, :]
        column, offset = (digits[i][k : k + 1, :per_device].astype(F32).astype(jnp.int32) for k in range(2))
        at_slot = jnp.where(slot == offset, 1.0, 0.0)
        found = jnp.dot(table, at_slot.astype(BF16), preferred_element_type=F32)
        target = jnp.zeros((1, per_device), F32)
        for j in range(count):
            value = found[2 * j : 2 * j + 1, :] * BASE + found[2 * j + 1 : 2 * j + 2, :]
            target = target + jnp.where((column ^ me) == j, value, 0.0)
        target_ref[:, i * channels : i * channels + per_device] = target.astype(jnp.int32)
        chosen = jnp.where(column == me, at_slot, 0.0).astype(BF16)
        cell = cell + jnp.dot(chosen, feats, preferred_element_type=F32)
    unit, norms = unit_rows(cell.astype(BF16))
    cell_ref[...] = unit
    norm_ref[...] = jnp.broadcast_to(norms, norm_ref.shape)


def products(left, right):
    return lax.dot_general(left, right, (((1,), (1,)), ((), ())), preferred_element_type=F32)


def affinity(product):
    return jnp.exp2(product * (math.log2(math.e) / HEAT))


def lanes_of(length):
    return math.gcd(length, 512)


def each_part(length, body):
    size = length if length <= 768 else math.gcd(length, 768)
    if size == length:
        body(0, size)
    else:
        pl.loop(0, length // size)(lambda i: body(pl.multiple_of(i * size, size), size))


def tiles(rows, lanes):
    for strip in range(0, rows, 16):
        yield strip, [
            [(slice(row, row + 8), slice(lane, lane + 128)) for row in range(strip, strip + 16, 8)]
            for lane in range(0, lanes, 128)
        ]


def gather_keys(blocks, whole_ref):
    per_device = blocks[0].shape[0]
    for i, block in enumerate(blocks):
        whole_ref[i * per_device : (i + 1) * per_device, :] = block[...]


def stat_kernel(count, qx_ref, qy_ref, *refs):
    key_ref, query_ref, kx_ref, ky_ref, sums_ref = refs[2 * count :]
    gather_keys(refs[:count], kx_ref)
    gather_keys(refs[count : 2 * count], ky_ref)
    keys, lanes = kx_ref.shape[0], lanes_of(qx_ref.shape[0])
    query_ref[...] = jnp.zeros_like(query_ref)

    def part(base, size):
        for start in range(0, qx_ref.shape[0], lanes):
            span = slice(start, start + lanes)
            x = products(kx_ref[pl.ds(base, size), :], qx_ref[span, :])
            y = products(ky_ref[pl.ds(base, size), :], qy_ref[span, :])
            query = [[0.0] * (lanes // 128) for _ in range(4)]
            for strip, columns in tiles(size, lanes):
                key = [[0.0] * 2 for _ in range(4)]
                for i, column in enumerate(columns):
                    for j, at in enumerate(column):
                        a, b = affinity(x[at]), affinity(y[at])
                        for k, value in enumerate((a, b, a * a, a * b)):
                            key[k][j] = key[k][j] + value
                            query[k][i] = query[k][i] + value
                for k in range(4):
                    for j in range(2):
                        rows = pl.ds(base + strip + 8 * j, 8)
                        if start:
                            sums_ref[k, rows, :] += key[k][j]
                        else:
                            sums_ref[k, rows, :] = key[k][j]
            for k in range(4):
                for i, value in enumerate(query[k]):
                    at = slice(start + i * 128, start + i * 128 + 128)
                    query_ref[k : k + 1, at] += jnp.sum(value, axis=0, keepdims=True)

    each_part(keys, part)
    key_ref[4:, :] = jnp.zeros_like(key_ref[4:, :])
    for k in range(4):
        for row in range(0, keys, 128):
            at = slice(row, row + 128)
            key_ref[k : k + 1, at] = jnp.sum(sums_ref[k, at, :].T, axis=0, keepdims=True)


def factors(sums, scale):
    render, target, square, cross = (sums[k : k + 1, :] for k in range(4))
    by_render, by_target = scale / render, scale / target
    mix = (square * by_render * by_render - cross * by_render * by_target) / scale
    return by_render * by_render, by_render * by_target, by_render * mix


def reorder(values, size, flip):
    blocks = values.shape[1] // size
    return jnp.concatenate(
        [values[:, (i ^ flip) * size : ((i ^ flip) + 1) * size] for i in range(blocks)], axis=1
    )


def sum_kernel(size, flip, own_ref, other_ref, out_ref):
    out_ref[...] = own_ref[...] + reorder(other_ref[...], size, flip)


def grad_kernel(count, chosen, rows, parts, scale, qx_ref, qy_ref, *refs):
    kx_blocks, ky_blocks, refs = refs[:count], refs[count : 2 * count], refs[2 * count :]
    key_sums, query_sums, refs = refs[:rows], refs[rows : rows + parts], refs[rows + parts :]
    outs = refs[:count]
    kx_ref, ky_ref, key_ref, query_ref, total_ref = refs[count:]
    per_device = kx_blocks[0].shape[0]
    gather_keys(kx_blocks, kx_ref)
    gather_keys(ky_blocks, ky_ref)
    sums = query_sums[0][...]
    for k in range(1, parts):
        sums = sums + reorder(query_sums[k][...], 2 * per_device, k)
    for k, row in enumerate(factors(sums, scale)):
        query_ref[k : k + 1, :] = row
    sums = key_sums[0][0:4, :]
    for k in range(1, rows):
        sums = sums + reorder(key_sums[k][0:4, :], per_device, k)
    wanted = sums[:, chosen * per_device : (chosen + count) * per_device]
    for k, row in enumerate(factors(wanted, scale)):
        key_ref[k] = jnp.broadcast_to(row, (128, row.shape[1])).T

    lanes = lanes_of(qx_ref.shape[0])

    def part(base, size):
        rows = pl.ds(base, size)
        for start in range(0, qx_ref.shape[0], lanes):
            span = slice(start, start + lanes)
            queries = qx_ref[span, :]
            x = products(kx_ref[rows, :], queries)
            y = products(ky_ref[rows, :], qy_ref[span, :])
            query = [
                [jnp.broadcast_to(query_ref[k : k + 1, i : i + 128], (8, 128)) for k in range(3)]
                for i in range(start, start + lanes, 128)
            ]
            weights = []
            for strip, columns in tiles(size, lanes):
                row = []
                for i, column in enumerate(columns):
                    pair = []
                    for j, at in enumerate(column):
                        a, b = affinity(x[at]), affinity(y[at])
                        group = pl.ds(base + strip + 8 * j, 8)
                        square, cross, single = (key_ref[k, group, :] + query[i][k] for k in range(3))
                        pair.append(a * (a * square - b * cross - single))
                    row.append(jnp.concatenate(pair, axis=0).astype(BF16))
                weights.append(jnp.concatenate(row, axis=1))
            share = jnp.dot(
                jnp.concatenate(weights, axis=0), queries, preferred_element_type=F32
            )
            if start:
                total_ref[rows, :] += share
            else:
                total_ref[rows, :] = share

    each_part(kx_ref.shape[0], part)
    for k, out in enumerate(outs):
        out[...] = total_ref[k * per_device : (k + 1) * per_device, :].astype(out.dtype)


def last_kernel(unit_ref, norm_ref, *refs):
    parts, (out_ref, held_ref, sems) = refs[:-3], refs[-3:]
    size = out_ref.shape[0] // sems.shape[0]
    copies = []
    for i in range(sems.shape[0]):
        rows = slice(i * size, (i + 1) * size)
        gradient = parts[0][rows, :]
        for part in parts[1:]:
            gradient = gradient + part[rows, :].astype(F32)
        unit = unit_ref[rows, :].astype(F32)
        along = jnp.sum(unit * gradient, axis=1, keepdims=True)
        held_ref[rows, :] = (gradient - unit * along) / norm_ref[rows, :1]
        at = pl.ds(i * size, size)
        copies.append(pltpu.make_async_copy(held_ref.at[at, :], out_ref.at[at, :], sems.at[i]))
        copies[-1].start()
    for copy in copies:
        copy.wait()


def call(kernel, out_shape, args, in_specs=None, scratch=(), mib=16, flops=0, nbytes=0, out_spec=VMEM):
    many = isinstance(out_shape, (tuple, list))
    return pl.pallas_call(
        kernel,
        out_shape=out_shape,
        in_specs=in_specs or [VMEM] * len(args),
        out_specs=[out_spec] * len(out_shape) if many else out_spec,
        scratch_shapes=scratch,
        compiler_params=params(mib),
        cost_estimate=pl.CostEstimate(flops=flops, bytes_accessed=nbytes, transcendentals=0),
    )(*args)


def body(ray_feat, ray_pos, target_index, target_map):
    per_device, channels = ray_feat.shape
    col_count = lax.axis_size("col")
    row_count = lax.axis_size("row")
    shape = jax.ShapeDtypeStruct
    queries, keys = col_count * per_device, row_count * per_device

    def flip(values, axis, bits):
        pairs = [(i, i ^ bits) for i in range(lax.axis_size(axis))]
        return lax.ppermute(values, axis, pairs)

    me = lax.axis_index("col").astype(jnp.int32).reshape(1)
    sent, own_list = call(
        functools.partial(send_kernel, col_count),
        (
            pltpu.VMEM((per_device + EXTRA, channels), BF16),
            pltpu.VMEM((1, channels), jnp.int32),
        ),
        (
            lax.axis_index("row").astype(jnp.int32).reshape(1),
            ray_feat,
            ray_pos.reshape(1, -1),
            target_index.reshape(1, -1),
        ),
        in_specs=[SMEM, HBM, HBM, HBM],
        scratch=[pltpu.VMEM((1, per_device), jnp.int32)] * 2 + [pltpu.SemaphoreType.DMA((3,))],
        mib=FULL,
    )
    own_target = call(
        own_target_kernel,
        shape((per_device, channels), BF16),
        (own_list, target_map),
        in_specs=[VMEM, HBM],
        scratch=table_scratch(target_map, per_device) + index_scratch(channels),
        mib=FULL - 8,
        nbytes=target_map.size * 2,
    )
    key_targets = [own_target] + [flip(own_target, "row", k) for k in range(1, row_count)]
    blocks = [sent, flip(sent, "col", 1)]
    for k in range(2, col_count, 2):
        block, own_target = lax.optimization_barrier((flip(sent, "col", k), own_target))
        if k == col_count - 2:
            for j in range(1, min(row_count, 3)):
                block, key_targets[j] = lax.optimization_barrier((block, key_targets[j]))
        blocks += [block, flip(block, "col", 1)]
    targets, own_unit, own_norm = call(
        functools.partial(pick_kernel, col_count),
        (
            shape((1, col_count * channels), jnp.int32),
            shape((per_device, channels), BF16),
            shape((per_device, 128), F32),
        ),
        (me, *blocks),
        in_specs=[SMEM] + [VMEM] * col_count,
        nbytes=queries * channels * 4,
    )
    key_units = [own_unit] + [flip(own_unit, "row", k) for k in range(1, row_count)]
    query_unit, query_target = call(
        functools.partial(query_kernel, col_count),
        [shape((queries, channels), BF16)] * 2,
        (targets, target_map, *blocks),
        in_specs=[VMEM, HBM] + [VMEM] * col_count,
        scratch=table_scratch(target_map, queries) + index_scratch(col_count * channels),
        mib=FULL - 10,
        nbytes=target_map.size * 2,
    )

    flops = 2 * queries * keys * channels
    key_scratch = [pltpu.VMEM((keys, channels), BF16)] * 2
    key_sums, query_sums = call(
        functools.partial(stat_kernel, row_count),
        (shape((KEY_ROWS, keys), F32), shape((4, queries), F32)),
        (query_unit, query_target, *key_units, *key_targets),
        scratch=key_scratch + [pltpu.VMEM((4, keys, 128), F32)],
        mib=32,
        flops=2 * flops,
    )
    for k in range(max(col_count, row_count).bit_length() - 1):
        if 1 << k < row_count:
            key_sums = call(
                functools.partial(sum_kernel, per_device, 1 << k),
                shape((KEY_ROWS, keys), F32),
                (key_sums, flip(key_sums, "row", 1 << k)),
            )
        if 1 << k < col_count:
            other = (2 << k) if (2 << k) < col_count else 1
            query_sums = call(
                functools.partial(sum_kernel, per_device, other),
                shape((4, queries), F32),
                (query_sums, flip(query_sums, "col", other)),
            )
    key_parts, query_parts = [key_sums], [query_sums]
    scale = float(queries * row_count) / math.sqrt(HEAT)

    def gradient(chosen, count, dtype, query_unit):
        return call(
            functools.partial(grad_kernel, count, chosen, 1, 1, scale),
            [shape((per_device, channels), dtype)] * count,
            (
                query_unit,
                query_target,
                *key_units[chosen : chosen + count],
                *key_targets[chosen : chosen + count],
                *key_parts,
                *query_parts,
            ),
            scratch=[pltpu.VMEM((count * per_device, channels), BF16)] * 2
            + [
                pltpu.VMEM((3, count * per_device, 128), F32),
                pltpu.VMEM((3, queries), F32),
                pltpu.VMEM((count * per_device, channels), F32),
            ],
            mib=32,
            flops=3 * flops * count // row_count,
        )

    partials, query_unit = lax.optimization_barrier(
        (gradient(1, row_count - 1, BF16, query_unit), query_unit)
    )
    (own_part,) = gradient(0, 1, F32, query_unit)
    partials = [own_part] + [flip(part, "row", k + 1) for k, part in enumerate(partials)]
    return call(
        last_kernel,
        shape((per_device, channels), F32),
        (own_unit, own_norm, *partials),
        scratch=[
            pltpu.VMEM((per_device, channels), F32),
            pltpu.SemaphoreType.DMA((math.gcd(per_device // 16, 3),)),
        ],
        out_spec=HBM,
    )


def solution(mesh):
    return jax.shard_map(
        body,
        mesh=mesh,
        in_specs=(P(("row", "col"), None), P(("row", "col")), P(("row", "col")), P()),
        out_specs=P(("row", "col"), None),
        check_vma=False,
    )
```
